256 devices in a mesh: fsdp: 64 (over z, y, core), group: 4 (over x).
Axes of the slice: x: 4, y: 4, z: 8, core: 2. Of those that a mesh axis runs over, the one named last changes fastest.
Arguments:
- grads: bfloat16 [56, 1024, 1024], P(None, 'fsdp', 'group'), may hold values from -0.29882812 to 0.29882812
- second_moment: float32 [56, 1024, 1024], P(None, 'fsdp', 'group'), may hold values from 0.0001 to 0.01
- slot_of: int32 [56], replicated, may hold values from 0 to 127, as said below
- block_rows: int32 [56], replicated, may hold values from 512 to 1024, as said below
- block_cols: int32 [56], replicated, may hold values from 512 to 1024, as said below
- left_stat: float32 [128, 1024, 1024], P('fsdp', 'group')
- right_stat: float32 [128, 1024, 1024], P('fsdp', 'group')
- left_root: bfloat16 [128, 1024, 1024], P('fsdp', 'group'), as said below
- right_root: bfloat16 [128, 1024, 1024], P('fsdp', None, 'group'), as said below
Outputs:
- directions: bfloat16 [56, 1024, 1024], P(None, 'fsdp', 'group')
- new_moment: float32 [56, 1024, 1024], P(None, 'fsdp', 'group')
- new_left: float32 [128, 1024, 1024], P('fsdp', 'group')
- new_right: float32 [128, 1024, 1024], P('fsdp', 'group')
The draws below stay inside these ranges and needn't reach their ends.
Inputs may be any that keep to these rules, and one draw needn't show every extreme that they name: slot_of holds distinct values; every owner (value // 2) receives at most 2 blocks, owner 0 receives exactly 2, and slot 127 always holds a block. `block_rows`: each value is B // 2 or 1024. `block_cols`: each value is B // 2 or 1024. `left_root`: each matrix is symmetric. `right_root`: each matrix is symmetric.
All inputs are finite; a program needn't handle non-finite values.
Results may differ from the reference program's by a relative error of at most 0.005.
Values may be sent and summed in bfloat16 or wider, within the bound.
A program may use at most 64 MiB of HBM per device.

```python
import math
import jax
import jax.numpy as jnp
from jax import lax

B = 1024
NBLK = 56
TOTAL_SLOTS = 128


def symmetric(key, noise, lower, upper):
    diagonal = jax.random.uniform(key, (TOTAL_SLOTS, B, 1), jnp.float32, lower, upper)
    ident = (jnp.arange(B)[:, None] == jnp.arange(B)[None, :]).astype(jnp.float32)
    return (noise + jnp.swapaxes(noise, 1, 2)) * 0.5 + ident[None] * diagonal


def rough_noise(key, factor):
    return jax.random.normal(key, (TOTAL_SLOTS, B, B), jnp.float32) * (factor / math.sqrt(B))


def draw_left_root(key, part):
    key = jax.random.fold_in(key, 31)
    first, second = jax.random.split(key)
    return symmetric(second, rough_noise(first, 1.0), 0.5, 1.5).astype(jnp.bfloat16)


def draw_right_root(key, part):
    key = jax.random.fold_in(key, 37)
    first, second = jax.random.split(key)
    return symmetric(second, rough_noise(first, 1.0), 0.5, 1.5).astype(jnp.bfloat16)


def draw_left_stat(key, part):
    key = jax.random.fold_in(key, 41)
    first, second = jax.random.split(key)
    return symmetric(second, rough_noise(first, 2.0), 1.0, 3.0)


def draw_right_stat(key, part):
    key = jax.random.fold_in(key, 43)
    first, second = jax.random.split(key)
    return symmetric(second, rough_noise(first, 2.0), 1.0, 3.0)


def draw_slot_of(key, part):
    key = jax.random.fold_in(key, 11)
    first, second = jax.random.split(key)
    others = jax.random.permutation(first, TOTAL_SLOTS - 3) + 2
    fixed = jnp.array([0, 1, TOTAL_SLOTS - 1], jnp.int32)
    chosen = jnp.concatenate([fixed, others[:NBLK - 3].astype(jnp.int32)])
    order = jax.random.permutation(second, NBLK)
    return chosen[order].astype(jnp.int32)


def edge_sizes(key):
    picks = jax.random.randint(key, (NBLK,), 0, 2)
    values = B // 2 + B // 2 * picks
    return values.at[0].set(B).at[1].set(B // 2).astype(jnp.int32)


def draw_block_rows(key, part):
    key = jax.random.fold_in(key, 21)
    return edge_sizes(key)


def draw_block_cols(key, part):
    key = jax.random.fold_in(key, 23)
    return edge_sizes(key)


def steps_of(rng, shape, cuts, low, high):
    def one(axis_at, blocks):
        steps = jax.random.uniform(jax.random.fold_in(jax.random.fold_in(rng, 6), axis_at), (blocks,), jnp.float32, low / len(cuts), high / len(cuts))
        return jnp.repeat(jnp.exp(steps), shape[axis_at] // blocks).reshape((-1,) + (1,) * (len(shape) - axis_at - 1))

    gain = one(*cuts[0])
    for cut in cuts[1:]:
        gain = gain * one(*cut)
    return gain


def scatter_about(stream_key, dims, width, reach, shards=(), kind=jnp.bfloat16):
    factor_of = steps_of(stream_key, dims, shards, -0.22, 0.18) if shards else 1.0
    entries = jax.random.normal(stream_key, dims, jnp.float32) * width * factor_of
    return jnp.minimum(jnp.maximum(entries, -reach), reach).astype(kind)


def setup_inputs(seed: int = 0) -> dict:
    streams_of = jax.random.split(jax.random.key(seed), 10)
    return {
        "grads": scatter_about(streams_of[0], (NBLK, B, B), 0.05, 0.29882812, ((1, 64), (2, 4))),
        "second_moment": jnp.clip(jnp.exp(math.log(0.01) - 4.6051702 * jax.random.uniform(streams_of[1], (NBLK, B, B), jnp.float32) ** steps_of(streams_of[1], (NBLK, B, B), ((1, 64), (2, 4)), -0.2, 0.2)), 0.0001, 0.01),
        "slot_of": draw_slot_of(jax.random.fold_in(streams_of[9], 71), 0),
        "block_rows": draw_block_rows(jax.random.fold_in(streams_of[9], 71), 0),
        "block_cols": draw_block_cols(jax.random.fold_in(streams_of[9], 71), 0),
        "left_stat": draw_left_stat(jax.random.fold_in(streams_of[9], 71), 0),
        "right_stat": draw_right_stat(jax.random.fold_in(streams_of[9], 71), 0),
        "left_root": draw_left_root(jax.random.fold_in(streams_of[9], 71), 0),
        "right_root": draw_right_root(jax.random.fold_in(streams_of[9], 71), 0),
    }


def reference(grads, second_moment, slot_of, block_rows, block_cols, left_stat, right_stat, left_root, right_root):
    index = jnp.arange(B, dtype=jnp.int32)
    mask = (index[None, :, None] < block_rows[:, None, None]) & (index[None, None, :] < block_cols[:, None, None])
    grad = jnp.where(mask, grads, jnp.zeros_like(grads))
    grad32 = grad.astype(jnp.float32)
    moment = 0.95 * second_moment + 0.05 * grad32 * grad32
    adam = grad32 / (jnp.sqrt(moment) + 1e-08)
    adam_norm = jnp.sqrt(lax.optimization_barrier(jnp.sum(adam * adam, axis=(1, 2))))

    def one_block(blk):
        piece = grad[blk]
        slot = slot_of[blk]
        gram_left = jnp.dot(piece, piece.T, preferred_element_type=jnp.float32)
        gram_right = jnp.dot(piece.T, piece, preferred_element_type=jnp.float32)
        mixed = jnp.dot(piece, right_root[slot], preferred_element_type=jnp.float32).astype(jnp.bfloat16)
        precond = jnp.dot(left_root[slot], mixed, preferred_element_type=jnp.float32)
        precond = jnp.where(mask[blk], precond, jnp.float32(0.0))
        precond_norm = jnp.sqrt(jnp.sum(precond * precond))
        direction = (precond * (adam_norm[blk] / (precond_norm + 1e-06))).astype(jnp.bfloat16)
        return (direction, gram_left, gram_right)
    directions, grams_left, grams_right = lax.map(one_block, jnp.arange(NBLK, dtype=jnp.int32))
    new_left = (0.9 * left_stat).at[slot_of].set(0.9 * left_stat[slot_of] + 0.1 * grams_left)
    new_right = (0.9 * right_stat).at[slot_of].set(0.9 * right_stat[slot_of] + 0.1 * grams_right)
    return (directions, moment, new_left, new_right)
```

```python
import jax
import jax.numpy as jnp
from jax import lax
from jax.experimental import pallas as pl
from jax.experimental.pallas import tpu as pltpu
from jax.sharding import PartitionSpec as P

MESH = pl.DeviceIdType.MESH
Z, Y, X = 8, 4, 4
QUADS = Z * Y
EDGE = 1024
NBLK = 56
HALF = EDGE // 2
ROWS, COLS = 16, 256


def drain(ref, sem):
    pltpu.make_async_copy(ref, ref, sem).wait()


def exchange(
    slot_ref,
    rows_ref,
    cols_ref,
    grads_ref,
    second_ref,
    lstat_ref,
    rstat_ref,
    lroot_ref,
    rroot_ref,
    returned,
    moment_ref,
    new_left_ref,
    new_right_ref,
    moments,
    new_left,
    new_right,
    grads,
    second,
    table,
    table_smem,
    pieces,
    gleft_in,
    gright_in,
    block,
    lroot,
    rroot,
    mixed,
    precond,
    direction,
    gleft,
    gright,
    relay,
    cross,
    half_way,
    by_x,
    by_z,
    adam_in,
    adam_sum,
    norm,
    block_send,
    block_recv,
    swap_send,
    swap_recv,
    root_send,
    root_recv,
    row_recv,
    pass_send,
    pass_recv,
    gram_send,
    gram_recv,
    relay_send,
    relay_recv,
    adam_send,
    adam_recv,
    norm_send,
    norm_recv,
    out_send,
    out_recv,
    bulk_send,
    pass_out_send,
    half_way_recv,
    by_x_recv,
    by_z_recv,
    load_sem,
    store_sem,
    table_sem,
):
    f = lax.axis_index("fsdp")
    g = lax.axis_index("group")
    core = lax.rem(f, 2)
    quad = lax.div(f, 2)
    y = lax.rem(quad, Y)
    z = lax.div(quad, Y)
    slot = quad * X + g
    other = f + 1 - 2 * core
    side = lax.div(g, 2)
    parity = lax.rem(g, 2)
    at_home = side == core

    def device(zz, yy, cc):
        return (zz * Y + yy) * 2 + cc

    def remote(src, dst, send, recv, ff, gg):
        pltpu.make_async_remote_copy(
            src_ref=src,
            dst_ref=dst,
            send_sem=send,
            recv_sem=recv,
            device_id=(ff, gg),
            device_id_type=MESH,
        ).start()

    def span(j):
        return pl.ds(pl.multiple_of(lax.rem(j, X) * COLS, COLS), COLS)

    def left_block(ref, j, k):
        return ref.at[span(j), span(k)]

    def send_root(k, ff, xx, lefts, rights):
        for d in lefts:
            src = lroot_ref.at[k, :, span(g + d)]
            remote(src, left_block(lroot, g, g + d), root_send.at[k], root_recv, ff, xx)
        for d in rights:
            src = rroot_ref.at[k, span(g + d), :]
            remote(src, left_block(rroot, g + d, g), root_send.at[k], root_recv, ff, xx)

    for k in range(2):
        home = 2 * core + k
        around = lax.rem(g - home + X, X)

        @pl.when(around == 0)
        def _():
            for src, dst in ((lroot_ref.at[k], lroot.at[span(g)]), (rroot_ref.at[k], rroot.at[:, span(g)])):
                remote(src, dst, root_send.at[k], row_recv, other, g)
                pltpu.make_async_copy(src, dst, row_recv).start()

        @pl.when(around == 1)
        def _():
            send_root(k, quad * 2, home, (0, 1, 2), (0, 1))

        @pl.when(around == 2)
        def _():
            send_root(k, quad * 2, home, (0,), ())
            send_root(k, quad * 2 + 1, home, (), (0,))

        @pl.when(around == 3)
        def _():
            send_root(k, quad * 2 + 1, home, (0, 3), (0, 3, 2))

    load_grads = pltpu.make_async_copy(grads_ref, grads.at[pl.ds(0, NBLK)], load_sem.at[0])
    load_second = pltpu.make_async_copy(second_ref, second, load_sem.at[1])
    load_left = pltpu.make_async_copy(lstat_ref, new_left, load_sem.at[2])
    load_right = pltpu.make_async_copy(rstat_ref, new_right, load_sem.at[3])
    load_grads.start()
    load_second.start()
    lane = lax.broadcasted_iota(jnp.int32, (8, 128), 1)

    def valid(b):
        return (f * ROWS < rows_ref[b]) & (g * COLS < cols_ref[b])

    source = jnp.full((8, 128), NBLK, jnp.int32)
    for b in range(NBLK):
        source = jnp.where(lane == slot_ref[b], jnp.where(valid(b), b, NBLK), source)
    table[...] = source
    to_smem = pltpu.make_async_copy(table, table_smem, table_sem)
    to_smem.start()
    grads[NBLK] = jnp.zeros((ROWS, COLS), jnp.bfloat16)
    to_smem.wait()
    load_grads.wait()

    mine = block.at[quad, core, :, pl.ds(pl.multiple_of(g * COLS, COLS), COLS)]

    def fill(at):
        pieces[at] = grads[table_smem[0, at]]

    across = lax.rem(z + Z // 2, Z) * Y * X
    for way, ff in ((0, device(lax.rem(z + 2, Z), y, core)), (1, device(lax.rem(z + 6, Z), y, core))):
        for n in range(8):
            fill(across + way * 8 + n)
        bulk = pieces.at[pl.ds(across + way * 8, 8)]
        remote(bulk, half_way.at[way], bulk_send, half_way_recv.at[way], ff, g)

    def send_blocks(step, carry):
        dy, dx = lax.div(step, X), lax.rem(step, X)
        yy, xx = lax.rem(y + dy, Y), lax.rem(g + dx, X)
        for dz in (3, 5, 2, 6, 1, 7, 0):
            zz = lax.rem(z + dz, Z)
            at = (zz * Y + yy) * X + xx
            fill(at)
            src = pieces.at[at]
            if dz:
                remote(src, mine, block_send, block_recv, device(zz, yy, core), xx)
            else:

                @pl.when(step == 0)
                def _():
                    pltpu.make_async_copy(src, mine, block_recv).start()

                @pl.when(step != 0)
                def _():
                    remote(src, mine, block_send, block_recv, device(zz, yy, core), xx)

        return carry

    lax.fori_loop(0, X * Y, send_blocks, 0)

    for way in range(2):
        zz, zs = lax.rem(z + (2, 6)[way], Z), lax.rem(z + (6, 2)[way], Z)
        drain(half_way.at[way], half_way_recv.at[way])

        @pl.loop(0, 8)
        def _(n):
            dst = block.at[zs * Y + y, core, :, pl.ds(pl.multiple_of(g * COLS, COLS), COLS)]
            ff = device(zz, 2 * way + lax.div(n, X), core)
            remote(half_way.at[way, n], dst, block_send, block_recv, ff, lax.rem(n, X))

    def pass_on(ref, j, k):
        here = left_block(ref, j, k)
        remote(here, here, pass_send, pass_recv, other, g)

    load_left.start()
    load_right.start()

    load_second.wait()

    def one_block(b, sums):
        grad = jnp.where(valid(b), grads[b].astype(jnp.float32), 0.0)
        moment = 0.95 * second[b] + 0.05 * grad * grad
        moments[b] = moment
        adam = grad / (jnp.sqrt(moment) + 1e-08)
        adam = adam * adam
        adam = adam[0:8] + adam[8:16]
        adam = jnp.sum(adam[:, 0:128] + adam[:, 128:256], keepdims=True)
        return sums + jnp.where(lane == slot_ref[b], adam, 0.0)

    adam_sum[0] = lax.fori_loop(0, NBLK, one_block, jnp.zeros((8, 128), jnp.float32), unroll=4)

    store_moment = pltpu.make_async_copy(moments, moment_ref, store_sem.at[0])
    store_moment.start()

    def adam_stage(stage, first, peers):
        for d, (ff, gg) in enumerate(peers):
            remote(adam_sum.at[stage], adam_in.at[first + d], adam_send.at[stage], adam_recv.at[stage], ff, gg)

    def adam_add(stage, first, count):
        drain(adam_in.at[pl.ds(first, count)], adam_recv.at[stage])
        total = adam_sum[stage]
        for d in range(count):
            total = total + adam_in[first + d]
        return total

    adam_stage(0, 0, [(other, g)])

    drain(lroot.at[pl.ds(0, 6 * COLS // X)], root_recv)

    @pl.when(core == 0)
    def _():
        for ref, j, k in ((lroot, 1, 1), (lroot, 1, 2), (lroot, 1, 3), (lroot, 2, 2), (rroot, 1, 1), (rroot, 2, 1)):
            pass_on(ref, g + j, g + k)

    @pl.when(core == 1)
    def _():
        for ref, j, k in ((lroot, 3, 3), (lroot, 3, 2), (rroot, 3, 3), (rroot, 2, 3), (rroot, 1, 3), (rroot, 2, 2)):
            pass_on(ref, g + j, g + k)

    adam_sum[1] = adam_add(0, 0, 1)
    adam_stage(1, 1, [(f, lax.rem(g + d, X)) for d in range(1, X)])

    drain(lroot.at[pl.ds(0, 2 * COLS)], row_recv)
    drain(lroot.at[pl.ds(0, 6 * COLS // X)], pass_recv)
    for j, k in ((1, 0), (2, 0), (3, 0), (2, 1), (2, 3), (1, 3)):
        rroot[span(g + k), span(g + j)] = rroot[span(g + j), span(g + k)].T
    for j, k in ((0, 1), (0, 2), (0, 3), (1, 2), (3, 2), (1, 3)):
        lroot[span(g + k), span(g + j)] = lroot[span(g + j), span(g + k)].T
    half = pl.ds(pl.multiple_of(core * HALF, HALF), HALF)

    drain(block.at[:, core], block_recv)
    remote(block.at[:, core], block.at[:, core], swap_send, swap_recv, other, g)

    def mix(cc):
        @pl.loop(0, 2)
        def _(m):
            at = pl.ds(pl.multiple_of(m * 16, 16), 16)
            part = block[at, cc].reshape(COLS, EDGE)
            value = jnp.dot(part, rroot[:, half], preferred_element_type=jnp.float32)
            mixed[at, cc] = value.astype(jnp.bfloat16).reshape(16, ROWS, HALF)

    mix(core)
    drain(block.at[:, 1 - core], swap_recv)

    def send_gram(which, m, src, dst):
        xx = 2 * core + m
        ff = quad * 2 + side
        around = lax.rem(xx - g + X, X)
        send = gram_send.at[which, m]

        @pl.when(around == 0)
        def _():
            pltpu.make_async_copy(src.at[m], dst.at[parity], gram_recv.at[which, parity]).start()

        @pl.when(lax.rem(around, 2) == 1)
        def _():
            remote(src.at[m], dst.at[parity], send, gram_recv.at[which, parity], ff, xx)

        @pl.when(around == 2)
        def _():
            for d, gg in ((0, lax.rem(g + 1, X)), (2, lax.rem(g + 3, X))):
                remote(src.at[m, :, span(g + d)], relay.at[which], send, relay_recv.at[which], ff, gg)

    def whole():
        return block[...].reshape(EDGE, EDGE)

    for m in range(2):
        part = block[pl.ds(core * 16 + m * 8, 8)].reshape(COLS, EDGE)
        gleft[m] = lax.dot_general(
            part, whole(), (((1,), (1,)), ((), ())), preferred_element_type=jnp.float32
        ).astype(jnp.bfloat16)
        send_gram(0, m, gleft, gleft_in)

    mix(1 - core)
    adam_sum[2] = adam_add(1, 1, X - 1)
    adam_stage(2, 4, [(device(z, lax.rem(y + d, Y), core), g) for d in range(1, Y)])

    rows_valid, cols_valid = 0, 0
    for b in range(NBLK):
        rows_valid = jnp.where(slot_ref[b] == slot, rows_ref[b], rows_valid)
        cols_valid = jnp.where(slot_ref[b] == slot, cols_ref[b], cols_valid)
    cols_keep = (core * HALF + lax.broadcasted_iota(jnp.int32, (COLS, HALF), 1)) < cols_valid

    def one_part(m, total):
        at = pl.multiple_of(m * COLS, COLS)
        value = jnp.dot(lroot[pl.ds(at, COLS)], mixed[...].reshape(EDGE, HALF), preferred_element_type=jnp.float32)
        rows_keep = (at + lax.broadcasted_iota(jnp.int32, (COLS, HALF), 0)) < rows_valid
        value = jnp.where(rows_keep & cols_keep, value, 0.0)
        precond[pl.ds(at, COLS)] = value
        square = value * value
        return total + jnp.sum(square.reshape(COLS // 8, 8, HALF), axis=0)

    total = lax.fori_loop(0, 4, one_part, jnp.zeros((8, HALF), jnp.float32))
    norm[0] = jnp.broadcast_to(jnp.sum(total, keepdims=True), (8, 128))
    remote(norm.at[0], norm.at[1], norm_send, norm_recv, other, g)

    adam_sum[3] = adam_add(2, 4, Y - 1)
    adam_stage(3, 7, [(device(lax.rem(z + d, Z), y, core), g) for d in range(1, Z)])

    for m in range(2):
        at = pl.multiple_of(core * HALF + m * COLS, COLS)
        part = block[:, :, :, pl.ds(at, COLS)].reshape(EDGE, COLS)
        gright[m] = lax.dot_general(
            part, whole(), (((0,), (0,)), ((), ())), preferred_element_type=jnp.float32
        ).astype(jnp.bfloat16)
        send_gram(1, m, gright, gright_in)

    adam = adam_add(3, 7, Z - 1)
    adam = jnp.sum(jnp.where(lane == slot, adam, 0.0)[0:1], keepdims=True)

    drain(norm.at[1], norm_recv)
    squares = (norm[0] + norm[1])[0:1, 0:1]
    factor = jnp.sqrt(adam) / (jnp.sqrt(squares) + 1e-06)

    @pl.loop(0, 4)
    def _(m):
        at = pl.multiple_of(m * COLS, COLS)
        value = (precond[pl.ds(at, COLS)] * factor).astype(jnp.bfloat16)
        direction[pl.ds(m * 16, 16)] = value.reshape(16, ROWS, HALF)

    def columns(e):
        return pl.ds(pl.multiple_of(e * COLS, COLS), COLS)

    def tie(e):
        return lax.rem(2 * core + e - g + X, X) == 2

    for e in range(2):

        @pl.when(tie(e))
        def _():
            for n, gg in ((0, lax.rem(g + 1, X)), (1, lax.rem(g + 3, X))):
                src = direction.at[pl.ds(n * QUADS, QUADS), :, columns(e)]
                remote(src, by_x, bulk_send, by_x_recv, f, gg)

    for e in range(2):

        @pl.when(jnp.logical_not(tie(e)))
        def _():
            for way, dz in ((0, 2), (1, 6)):
                src = direction.at[pl.ds(lax.rem(z + 4, Z) * 8 + way * 4, 4), :, columns(e)]
                ff = device(lax.rem(z + dz, Z), y, core)
                remote(src, by_z.at[way, e], bulk_send, by_z_recv.at[way, e], ff, g)

    def send_out(step, carry):
        dy, dc = lax.div(step, 2), lax.rem(step, 2)
        yy, cc = lax.rem(y + dy, Y), lax.rem(core + dc, 2)
        for e in range(2):
            xx = 2 * core + e

            @pl.when(jnp.logical_not(tie(e)))
            def _():
                for dz in (3, 5, 2, 6, 1, 7, 0):
                    ff = device(lax.rem(z + dz, Z), yy, cc)
                    src = direction.at[ff, :, columns(e)]
                    dst = returned.at[slot]
                    if dz:
                        remote(src, dst, out_send, out_recv, ff, xx)
                    else:
                        local = (step == 0) & (xx == g)

                        @pl.when(local)
                        def _():
                            pltpu.make_async_copy(src, dst, out_recv).start()

                        @pl.when(jnp.logical_not(local))
                        def _():
                            remote(src, dst, out_send, out_recv, ff, xx)

        return carry

    lax.fori_loop(0, 8, send_out, 0)

    drain(by_x, by_x_recv)
    left_neighbour = lax.rem(g + 3, X)
    from_left = lax.div(left_neighbour, 2) != core
    origin = jnp.where(from_left, left_neighbour, lax.rem(g + 1, X))
    first = jnp.where(from_left, 0, QUADS)

    def on_x(n, carry):
        at = lax.rem(n + quad, QUADS)
        remote(by_x.at[at], returned.at[quad * X + origin], pass_out_send, out_recv, first + at, lax.rem(origin + 2, X))
        return carry

    lax.fori_loop(0, QUADS, on_x, 0)

    for e in range(2):

        @pl.when(jnp.logical_not(tie(e)))
        def _():
            for way in range(2):
                zz, zs = lax.rem(z + (2, 6)[way], Z), lax.rem(z + (6, 2)[way], Z)
                drain(by_z.at[way, e], by_z_recv.at[way, e])

                @pl.loop(0, 4)
                def _(n):
                    dst = returned.at[(zs * Y + y) * X + g]
                    remote(by_z.at[way, e, n], dst, pass_out_send, out_recv, zz * 8 + way * 4 + n, 2 * core + e)

    arounds = [lax.rem(g - 2 * core - k + X, X) for k in range(2)]
    for which, gram in ((0, gleft_in), (1, gright_in)):
        for k in range(2):
            for way in (1, 3):

                @pl.when(arounds[k] == way)
                def _():
                    drain(gram.at[k], gram_recv.at[which, k])
                    drain(relay.at[which], relay_recv.at[which])
                    gg = lax.rem(g + way, X)
                    here = gram.at[k, :, span(g + way)]
                    send = relay_send.at[which]
                    recv = gram_recv.at[which, k]
                    remote(here, cross.at[which, way // 2], send, recv, f, gg)
                    column = span(g + 3)
                    remote(relay.at[which], gram.at[k, :, column], send, recv, f, gg)

    def update(target, gram, k):
        @pl.loop(0, 8)
        def _(m):
            at = pl.ds(pl.multiple_of(m * 32, 32), 32)
            target[k, at] = 0.9 * target[k, at] + 0.1 * gram[k, at].astype(jnp.float32)

    store_left = [pltpu.make_async_copy(new_left.at[k], new_left_ref.at[k], store_sem.at[1 + k]) for k in range(2)]
    store_right = [pltpu.make_async_copy(new_right.at[k], new_right_ref.at[k], store_sem.at[3 + k]) for k in range(2)]
    parts = ((0, new_left, gleft_in, store_left), (1, new_right, gright_in, store_right))
    load_left.wait()
    load_right.wait()
    for last in (False, True):
        for which, target, gram, store in parts:
            for k in range(2):

                @pl.when((arounds[k] == 2) == last)
                def _():
                    if last:
                        drain(gram.at[k], gram_recv.at[which, k])
                        gram[k, :, span(g + 3)] = cross[which, 0].T
                        gram[k, :, span(g + 1)] = cross[which, 1].T
                    else:

                        @pl.when(arounds[k] == 0)
                        def _():
                            drain(gram.at[k], gram_recv.at[which, k])

                    update(target, gram, k)
                    store[k].start()

    drain(pieces.at[pl.ds(0, QUADS * X - 1)], block_send)
    drain(block.at[:, core], swap_send)
    drain(lroot.at[pl.ds(0, 6 * COLS // X)], pass_send)
    drain(norm.at[0], norm_send)
    drain(adam_in.at[0], adam_send.at[0])
    drain(adam_in.at[pl.ds(0, 3)], adam_send.at[1])
    drain(adam_in.at[pl.ds(0, 3)], adam_send.at[2])
    drain(adam_in.at[pl.ds(0, 7)], adam_send.at[3])
    for k in range(2):
        around = lax.rem(g - 2 * core - k + X, X)
        for steps, blocks in ((0, 8), (1, 5), (2, 2), (3, 5)):

            @pl.when(around == steps)
            def _():
                drain(lroot.at[pl.ds(0, blocks * COLS // X)], root_send.at[k])

        around = lax.rem(2 * core + k - g + X, X)
        for which in range(2):

            @pl.when(lax.rem(around, 2) == 1)
            def _():
                drain(gleft.at[k], gram_send.at[which, k])

            @pl.when(around == 2)
            def _():
                drain(relay, gram_send.at[which, k])

    for which in range(2):
        drain(relay, relay_send.at[which])

    @pl.when(at_home)
    def _():
        drain(pieces.at[pl.ds(0, 2 * 56 - 1)], out_send)
        drain(pieces.at[pl.ds(0, 32 + 16)], pass_out_send)
        drain(pieces.at[pl.ds(0, 16 + 16)], bulk_send)

    @pl.when(jnp.logical_not(at_home))
    def _():
        drain(pieces.at[pl.ds(0, 56)], out_send)
        drain(pieces.at[pl.ds(0, 32 + 8)], pass_out_send)
        drain(pieces.at[pl.ds(0, 16 + 64 + 8)], bulk_send)

    drain(returned, out_recv)

    store_moment.wait()
    for store in store_left + store_right:
        store.wait()


def hand_over(
    slot_ref,
    returned,
    moment_in,
    left_in,
    right_in,
    directions,
    moment,
    left,
    right,
    left_held,
    right_held,
    moment_held,
    held,
    in_sem,
    out_sem,
    piece_sem,
):
    @pl.loop(0, NBLK)
    def _(b):
        pltpu.make_async_copy(returned.at[slot_ref[b]], held.at[b], piece_sem.at[0]).start()

    steps = []
    for src, kept, dst, count in (
        (left_in, left_held, left, 4),
        (right_in, right_held, right, 4),
        (moment_in, moment_held, moment, 2),
    ):
        size = dst.shape[0] // count
        for n in range(count):
            at = pl.ds(n * size, size)
            load = pltpu.make_async_copy(src.at[at], kept.at[at], in_sem.at[len(steps)])
            store = pltpu.make_async_copy(kept.at[at], dst.at[at], out_sem.at[len(steps)])
            load.start()
            steps.append((load, store))
    drain(held, piece_sem.at[0])
    last = pltpu.make_async_copy(held, directions, piece_sem.at[1])
    last.start()
    for load, store in steps:
        load.wait()
        store.start()
    for _, store in steps:
        store.wait()
    last.wait()


def run_exchange(grads, second_moment, slot_of, block_rows, block_cols, *matrices):
    half = jnp.bfloat16
    away = pl.BlockSpec(memory_space=pl.ANY)
    numbers = pl.BlockSpec(memory_space=pltpu.SMEM)
    dma = pltpu.SemaphoreType.DMA
    returned, moment, left, right = pl.pallas_call(
        exchange,
        out_shape=(
            jax.ShapeDtypeStruct((QUADS * X, ROWS, COLS), half),
            jax.ShapeDtypeStruct((NBLK, ROWS, COLS), jnp.float32),
            jax.ShapeDtypeStruct((2, COLS, EDGE), jnp.float32),
            jax.ShapeDtypeStruct((2, COLS, EDGE), jnp.float32),
        ),
        in_specs=[numbers] * 3 + [away] * 6,
        out_specs=(away, away, away, away),
        scratch_shapes=[
            pltpu.VMEM((NBLK, ROWS, COLS), jnp.float32),
            pltpu.VMEM((2, COLS, EDGE), jnp.float32),
            pltpu.VMEM((2, COLS, EDGE), jnp.float32),
            pltpu.VMEM((NBLK + 1, ROWS, COLS), half),
            pltpu.VMEM((NBLK, ROWS, COLS), jnp.float32),
            pltpu.VMEM((8, 128), jnp.int32),
            pltpu.SMEM((8, 128), jnp.int32),
            pltpu.VMEM((QUADS * X, ROWS, COLS), half),
            pltpu.VMEM((2, COLS, EDGE), half),
            pltpu.VMEM((2, COLS, EDGE), half),
            pltpu.VMEM((QUADS, 2, ROWS, EDGE), half),
            pltpu.VMEM((EDGE, EDGE), half),
            pltpu.VMEM((EDGE, EDGE), half),
            pltpu.VMEM((QUADS, 2, ROWS, HALF), half),
            pltpu.VMEM((EDGE, HALF), jnp.float32),
            pltpu.VMEM((QUADS * 2, ROWS, HALF), half),
            pltpu.VMEM((2, COLS, EDGE), half),
            pltpu.VMEM((2, COLS, EDGE), half),
            pltpu.VMEM((2, COLS, COLS), half),
            pltpu.VMEM((2, 2, COLS, COLS), half),
            pltpu.VMEM((2, 8, ROWS, COLS), half),
            pltpu.VMEM((QUADS, ROWS, COLS), half),
            pltpu.VMEM((2, 2, 4, ROWS, COLS), half),
            pltpu.VMEM((14, 8, 128), jnp.float32),
            pltpu.VMEM((4, 8, 128), jnp.float32),
            pltpu.VMEM((2, 8, 128), jnp.float32),
            dma,
            dma,
            dma,
            dma,
            dma((2,)),
            dma,
            dma,
            dma,
            dma,
            dma((2, 2)),
            dma((2, 2)),
            dma((2,)),
            dma((2,)),
            dma((4,)),
            dma((4,)),
            dma,
            dma,
            dma,
            dma,
            dma,
            dma,
            dma((2,)),
            dma,
            dma((2, 2)),
            dma((4,)),
            dma((5,)),
            dma,
        ],
        compiler_params=pltpu.CompilerParams(
            has_side_effects=True, vmem_limit_bytes=56 * 1024 * 1024
        ),
        cost_estimate=pl.CostEstimate(
            flops=8 * EDGE * EDGE * HALF, bytes_accessed=8 * EDGE * EDGE, transcendentals=0
        ),
    )(slot_of, block_rows, block_cols, grads, second_moment, *matrices)
    rows = (2 * COLS, EDGE)
    directions, moment, left, right = pl.pallas_call(
        hand_over,
        out_shape=(
            jax.ShapeDtypeStruct(grads.shape, half),
            jax.ShapeDtypeStruct(moment.shape, moment.dtype),
            jax.ShapeDtypeStruct(rows, left.dtype),
            jax.ShapeDtypeStruct(rows, right.dtype),
        ),
        in_specs=[numbers] + [away] * 4,
        out_specs=(away, away, away, away),
        scratch_shapes=[
            pltpu.VMEM(rows, left.dtype),
            pltpu.VMEM(rows, right.dtype),
            pltpu.VMEM(moment.shape, moment.dtype),
            pltpu.VMEM(grads.shape, half),
            dma((10,)),
            dma((10,)),
            dma((2,)),
        ],
        compiler_params=pltpu.CompilerParams(vmem_limit_bytes=56 * 1024 * 1024),
    )(slot_of, returned, moment, left.reshape(rows), right.reshape(rows))
    shape = matrices[0].shape
    return directions, moment, left.reshape(shape), right.reshape(shape)


def solution(mesh):
    placed = (
        P(None, "fsdp", "group"),
        P(None, "fsdp", "group"),
        P(),
        P(),
        P(),
        P("fsdp", "group", None),
        P("fsdp", "group", None),
        P("fsdp", "group", None),
        P("fsdp", None, "group"),
    )
    return jax.shard_map(
        run_exchange,
        mesh=mesh,
        in_specs=placed,
        out_specs=(
            P(None, "fsdp", "group"),
            P(None, "fsdp", "group"),
            P("fsdp", "group", None),
            P("fsdp", "group", None),
        ),
        check_vma=False,
    )
```

```python
import jax
import jax.numpy as jnp
from jax import lax
from jax.experimental import pallas as pl
from jax.experimental.pallas import tpu as pltpu
from jax.sharding import PartitionSpec as P

MESH = pl.DeviceIdType.MESH
Z, Y, X = 8, 4, 4
QUADS = Z * Y
EDGE = 1024
NBLK = 56
HALF = EDGE // 2
ROWS, COLS = 16, 256
FAR_FIRST = (4, 3, 5, 2, 6, 1, 7, 0)


def drain(ref, sem):
    pltpu.make_async_copy(ref, ref, sem).wait()


def exchange(
    slot_ref,
    rows_ref,
    cols_ref,
    grads_ref,
    second_ref,
    lstat_ref,
    rstat_ref,
    lroot_ref,
    rroot_ref,
    directions_ref,
    moment_ref,
    new_left_ref,
    new_right_ref,
    returned,
    directions,
    moments,
    new_left,
    new_right,
    grads,
    second,
    table,
    table_smem,
    matches,
    adam_parts,
    pieces,
    gleft_in,
    gright_in,
    block,
    lroot,
    rroot,
    mixed,
    precond,
    direction,
    gleft,
    gright,
    gram_part,
    relay,
    cross,
    adam_in,
    adam_sum,
    norm,
    block_send,
    block_recv,
    swap_send,
    swap_recv,
    root_send,
    root_recv,
    row_recv,
    pass_send,
    pass_recv,
    gram_send,
    gram_recv,
    relay_send,
    relay_recv,
    adam_send,
    adam_recv,
    norm_send,
    norm_recv,
    out_send,
    out_recv,
    load_sem,
    store_sem,
    table_sem,
):
    f = lax.axis_index("fsdp")
    g = lax.axis_index("group")
    core = lax.rem(f, 2)
    quad = lax.div(f, 2)
    y = lax.rem(quad, Y)
    z = lax.div(quad, Y)
    slot = quad * X + g
    other = f + 1 - 2 * core
    side = lax.div(g, 2)
    parity = lax.rem(g, 2)
    at_home = side == core

    def device(zz, yy, cc):
        return (zz * Y + yy) * 2 + cc

    def remote(src, dst, send, recv, ff, gg):
        pltpu.make_async_remote_copy(
            src_ref=src,
            dst_ref=dst,
            send_sem=send,
            recv_sem=recv,
            device_id=(ff, gg),
            device_id_type=MESH,
        ).start()

    def span(j):
        return pl.ds(pl.multiple_of(lax.rem(j, X) * COLS, COLS), COLS)

    def left_block(ref, j, k):
        return ref.at[span(j), span(k)]

    def send_rows():
        for k in range(2):

            @pl.when(lax.rem(g - 2 * core - k + X, X) == 0)
            def _():
                for src, dst in (
                    (lroot_ref.at[k], lroot.at[span(g)]),
                    (rroot_ref.at[k], rroot.at[:, span(g)]),
                ):
                    remote(src, dst, root_send.at[k], row_recv, other, g)
                    pltpu.make_async_copy(src, dst, row_recv).start()

    PLAN = (
        (1, 0, (((), (0, 1)), ((0, 1), ()), ((2,), ()))),
        (2, 0, (((), ()), ((0,), ()), ((), ()))),
        (2, 1, (((), (0,)), ((), ()), ((), ()))),
        (3, 1, (((), (0, 3)), ((0,), (2,)), ((3,), ()))),
    )

    def send_roots(turn, quarter):
        at = pl.multiple_of(quarter * 64, 64)
        for k in range(2):
            home = 2 * core + k
            for steps, cc, turns in PLAN:
                lefts, rights = turns[turn]
                if lefts or rights:

                    @pl.when(lax.rem(g - home + X, X) == steps)
                    def _():
                        for d in lefts:
                            src = lroot_ref.at[k, pl.ds(at, 64), span(g + d)]
                            dst = lroot.at[pl.ds(pl.multiple_of(g * COLS + at, 64), 64), span(g + d)]
                            remote(src, dst, root_send.at[k], root_recv, quad * 2 + cc, home)
                        for d in rights:
                            row = pl.ds(pl.multiple_of(lax.rem(g + d, X) * COLS + at, 64), 64)
                            src = rroot_ref.at[k, row, :]
                            remote(src, rroot.at[row, span(g)], root_send.at[k], root_recv, quad * 2 + cc, home)

    load_grads = pltpu.make_async_copy(grads_ref, grads.at[pl.ds(0, NBLK)], load_sem.at[0])
    load_second = pltpu.make_async_copy(second_ref, second, load_sem.at[1])
    load_left = pltpu.make_async_copy(lstat_ref, new_left, load_sem.at[2])
    load_right = pltpu.make_async_copy(rstat_ref, new_right, load_sem.at[3])
    load_grads.start()
    load_second.start()
    lane = lax.broadcasted_iota(jnp.int32, (8, 128), 1)

    def valid(b):
        return (f * ROWS < rows_ref[b]) & (g * COLS < cols_ref[b])

    source = jnp.full((8, 128), NBLK, jnp.int32)
    for b in range(NBLK):
        match = lane == slot_ref[b]
        source = jnp.where(match, jnp.where(valid(b), b, NBLK), source)
        matches[pl.ds(b, 1)] = match[0:1].astype(jnp.int32)
    table[...] = source
    to_smem = pltpu.make_async_copy(table, table_smem, table_sem)
    to_smem.start()
    grads[NBLK] = jnp.zeros((ROWS, COLS), jnp.bfloat16)
    to_smem.wait()
    load_grads.wait()

    mine = block.at[z, y, core, :, pl.ds(pl.multiple_of(g * COLS, COLS), COLS)]

    @pl.loop(0, QUADS * X // 8)
    def _(n):
        for k in range(8):
            pieces[n * 8 + k] = grads[table_smem[0, n * 8 + k]]

    def send_blocks(dy):
        yy = lax.rem(y + dy, Y)

        def step(dx, carry):
            xx = lax.rem(g + dx, X)
            for dz in FAR_FIRST:
                zz = lax.rem(z + dz, Z)
                src = pieces.at[(zz * Y + yy) * X + xx]
                to = (src, mine, block_send, block_recv.at[dy], device(zz, yy, core), xx)
                if dy or dz:
                    remote(*to)
                else:

                    @pl.when(dx == 0)
                    def _():
                        pltpu.make_async_copy(src, mine, block_recv.at[dy]).start()

                    @pl.when(dx != 0)
                    def _():
                        remote(*to)

                if dz == 2 and dy < 3:
                    send_roots(dy, dx)
            return carry

        lax.fori_loop(0, X, step, 0)

    def adam_stage(stage, first, peers):
        for d, (ff, gg) in enumerate(peers):
            remote(adam_sum.at[stage], adam_in.at[first + d], adam_send.at[stage], adam_recv.at[stage], ff, gg)

    def adam_add(stage, first, count):
        drain(adam_in.at[pl.ds(first, count)], adam_recv.at[stage])
        total = adam_sum[stage]
        for d in range(count):
            total = total + adam_in[first + d]
        return total

    send_blocks(0)

    load_second.wait()

    def one_block(b, carry):
        grad = jnp.where(valid(b), grads[b].astype(jnp.float32), 0.0)
        moment = 0.95 * second[b] + 0.05 * grad * grad
        moments[b] = moment
        adam = grad / (jnp.sqrt(moment) + 1e-08)
        adam = adam * adam
        adam = adam[0:8] + adam[8:16]
        adam_parts[b] = adam[:, 0:128] + adam[:, 128:256]
        return carry

    lax.fori_loop(0, NBLK, one_block, 0, unroll=4)
    adam = jnp.sum(jnp.sum(adam_parts[...], axis=1), axis=1, keepdims=True)
    adam = jnp.where(matches[...] != 0, adam, 0.0)
    adam_sum[0] = jnp.broadcast_to(jnp.sum(adam, axis=0, keepdims=True), (8, 128))
    store_moment = pltpu.make_async_copy(moments, moment_ref, store_sem.at[0])
    store_moment.start()

    adam_stage(0, 0, [(other, g)])
    send_blocks(1)
    adam_sum[1] = adam_add(0, 0, 1)
    adam_stage(1, 1, [(f, lax.rem(g + d, X)) for d in range(1, X)])
    send_blocks(2)
    send_rows()
    adam_sum[2] = adam_add(1, 1, X - 1)
    adam_stage(2, 4, [(device(z, lax.rem(y + d, Y), core), g) for d in range(1, Y)])
    send_blocks(3)
    load_left.start()
    load_right.start()

    def pass_on(ref, j, k):
        here = left_block(ref, j, k)
        remote(here, here, pass_send, pass_recv, other, g)

    drain(lroot.at[pl.ds(0, 6 * COLS // X)], root_recv)

    @pl.when(core == 0)
    def _():
        for ref, j, k in ((lroot, 1, 1), (lroot, 1, 2), (lroot, 1, 3), (lroot, 2, 2), (rroot, 1, 1), (rroot, 2, 1)):
            pass_on(ref, g + j, g + k)

    @pl.when(core == 1)
    def _():
        for ref, j, k in ((lroot, 3, 3), (lroot, 3, 2), (rroot, 3, 3), (rroot, 2, 3), (rroot, 1, 3), (rroot, 2, 2)):
            pass_on(ref, g + j, g + k)

    adam_sum[3] = adam_add(2, 4, Y - 1)
    adam_stage(3, 7, [(device(lax.rem(z + d, Z), y, core), g) for d in range(1, Z)])

    drain(lroot.at[pl.ds(0, 2 * COLS)], row_recv)
    drain(lroot.at[pl.ds(0, 6 * COLS // X)], pass_recv)
    for j, k in ((1, 0), (2, 0), (3, 0), (2, 1), (2, 3), (1, 3)):
        rroot[span(g + k), span(g + j)] = rroot[span(g + j), span(g + k)].T
    for j, k in ((0, 1), (0, 2), (0, 3), (1, 2), (3, 2), (1, 3)):
        lroot[span(g + k), span(g + j)] = lroot[span(g + j), span(g + k)].T
    half = pl.ds(pl.multiple_of(core * HALF, HALF), HALF)

    def send_gram(which, m, src, dst, at, size):
        xx = 2 * core + m
        ff = quad * 2 + side
        around = lax.rem(xx - g + X, X)
        send = gram_send.at[which, m]
        rows = pl.ds(at if isinstance(at, int) else pl.multiple_of(at, 16), size)

        @pl.when(around == 0)
        def _():
            here, there = src.at[m, rows], dst.at[parity, rows]
            pltpu.make_async_copy(here, there, gram_recv.at[which, parity]).start()

        @pl.when(lax.rem(around, 2) == 1)
        def _():
            here, there = src.at[m, rows], dst.at[parity, rows]
            remote(here, there, send, gram_recv.at[which, parity], ff, xx)

        @pl.when(around == 2)
        def _():
            for d, gg in ((0, lax.rem(g + 1, X)), (2, lax.rem(g + 3, X))):
                here = src.at[m, rows, span(g + d)]
                remote(here, relay.at[which, rows], send, relay_recv.at[which], ff, gg)

    def swap(d):
        ys = lax.rem(y + Y - d, Y)
        rows = block.at[:, ys, core]
        drain(rows, block_recv.at[d])
        remote(rows, rows, swap_send, swap_recv.at[d], other, g)

    def group(d):
        ys = lax.rem(y + Y - d, Y)
        drain(block.at[:, ys, 1 - core], swap_recv.at[d])
        for m in range(2):
            at = pl.multiple_of(core * HALF + m * COLS, COLS)
            value = lax.dot_general(
                block[:, ys, :, :, pl.ds(at, COLS)].reshape(COLS, COLS),
                block[:, ys].reshape(COLS, EDGE),
                (((0,), (0,)), ((), ())),
                preferred_element_type=jnp.float32,
            )
            if d:
                value = gram_part[m] + value
            if d < Y - 1:
                gram_part[m] = value
            else:
                gright[m] = value.astype(jnp.bfloat16)
                send_gram(1, m, gright, gright_in, 0, 128)
        value = jnp.dot(
            block[:, ys].reshape(COLS, EDGE), rroot[:, half], preferred_element_type=jnp.float32
        )
        mixed[:, ys] = value.astype(jnp.bfloat16).reshape(Z, 2, ROWS, HALF)

    swap(0)
    swap(1)
    group(0)
    swap(2)
    group(1)
    swap(3)
    group(2)
    group(3)

    rows_valid, cols_valid = 0, 0
    for b in range(NBLK):
        rows_valid = jnp.where(slot_ref[b] == slot, rows_ref[b], rows_valid)
        cols_valid = jnp.where(slot_ref[b] == slot, cols_ref[b], cols_valid)
    cols_keep = (core * HALF + lax.broadcasted_iota(jnp.int32, (COLS, HALF), 1)) < cols_valid

    def one_part(m, total):
        at = pl.multiple_of(m * COLS, COLS)
        value = jnp.dot(lroot[pl.ds(at, COLS)], mixed[...].reshape(EDGE, HALF), preferred_element_type=jnp.float32)
        rows_keep = (at + lax.broadcasted_iota(jnp.int32, (COLS, HALF), 0)) < rows_valid
        value = jnp.where(rows_keep & cols_keep, value, 0.0)
        precond[pl.ds(at, COLS)] = value
        square = value * value
        return total + jnp.sum(square.reshape(COLS // 8, 8, HALF), axis=0)

    total = lax.fori_loop(0, 4, one_part, jnp.zeros((8, HALF), jnp.float32))
    norm[0] = jnp.broadcast_to(jnp.sum(total, keepdims=True), (8, 128))
    remote(norm.at[0], norm.at[1], norm_send, norm_recv, other, g)

    for m in range(2):
        gleft[m] = lax.dot_general(
            block[pl.ds(core * 4 + m * 2, 2)].reshape(COLS, EDGE),
            block[...].reshape(EDGE, EDGE),
            (((1,), (1,)), ((), ())),
            preferred_element_type=jnp.float32,
        ).astype(jnp.bfloat16)

    adam = adam_add(3, 7, Z - 1)
    adam = jnp.sum(jnp.where(lane == slot, adam, 0.0)[0:1], keepdims=True)

    drain(norm.at[1], norm_recv)
    squares = (norm[0] + norm[1])[0:1, 0:1]
    factor = jnp.sqrt(adam) / (jnp.sqrt(squares) + 1e-06)

    @pl.loop(0, 4)
    def _(m):
        at = pl.multiple_of(m * COLS, COLS)
        value = (precond[pl.ds(at, COLS)] * factor).astype(jnp.bfloat16)
        direction[pl.ds(m * 16, 16)] = value.reshape(16, ROWS, HALF)

    def send_out(step, carry):
        dy, dc, e = lax.div(step, 4), lax.rem(lax.div(step, 2), 2), lax.rem(step, 2)
        yy, cc, xx = lax.rem(y + dy, Y), lax.rem(core + dc, 2), 2 * core + e
        for dz in FAR_FIRST:
            ff = device(lax.rem(z + dz, Z), yy, cc)
            src = direction.at[ff, :, pl.ds(pl.multiple_of(e * COLS, COLS), COLS)]
            dst = returned.at[slot]
            if dz:
                remote(src, dst, out_send, out_recv, ff, xx)
            else:
                local = (step < 2) & at_home & (parity == e)

                @pl.when(local)
                def _():
                    pltpu.make_async_copy(src, dst, out_recv).start()

                @pl.when(jnp.logical_not(local))
                def _():
                    remote(src, dst, out_send, out_recv, ff, xx)

            if dz in (3, 6):
                m = 0 if dz == 3 else 1
                send_gram(0, m, gleft, gleft_in, step * 16, 16)

            if dz in (2, 7):
                m = 0 if dz == 2 else 1

                @pl.when(lax.rem(step, 2) == 0)
                def _():
                    send_gram(1, m, gright, gright_in, 128 + step * 8, 16)

        return carry

    lax.fori_loop(0, 16, send_out, 0)

    arounds = [lax.rem(g - 2 * core - k + X, X) for k in range(2)]
    for which, gram in ((1, gright_in), (0, gleft_in)):
        for k in range(2):
            for way in (1, 3):

                @pl.when(arounds[k] == way)
                def _():
                    drain(gram.at[k], gram_recv.at[which, k])
                    drain(relay.at[which], relay_recv.at[which])
                    gg = lax.rem(g + way, X)
                    here = gram.at[k, :, span(g + way)]
                    send = relay_send.at[which]
                    recv = gram_recv.at[which, k]
                    remote(here, cross.at[which, way // 2], send, recv, f, gg)
                    column = span(g + 3)
                    remote(relay.at[which], gram.at[k, :, column], send, recv, f, gg)

    def update(target, gram, k):
        @pl.loop(0, 8)
        def _(m):
            at = pl.ds(pl.multiple_of(m * 32, 32), 32)
            target[k, at] = 0.9 * target[k, at] + 0.1 * gram[k, at].astype(jnp.float32)

    store_left = [pltpu.make_async_copy(new_left.at[k], new_left_ref.at[k], store_sem.at[1 + k]) for k in range(2)]
    store_right = [pltpu.make_async_copy(new_right.at[k], new_right_ref.at[k], store_sem.at[3 + k]) for k in range(2)]
    parts = ((1, new_right, gright_in, store_right), (0, new_left, gleft_in, store_left))
    load_left.wait()
    load_right.wait()
    for last in (False, True):
        for which, target, gram, store in parts:
            for k in range(2):

                @pl.when((arounds[k] == 2) == last)
                def _():
                    if last:
                        drain(gram.at[k], gram_recv.at[which, k])
                        gram[k, :, span(g + 3)] = cross[which, 0].T
                        gram[k, :, span(g + 1)] = cross[which, 1].T
                    else:

                        @pl.when(arounds[k] == 0)
                        def _():
                            drain(gram.at[k], gram_recv.at[which, k])

                    update(target, gram, k)
                    store[k].start()

    drain(pieces.at[pl.ds(0, QUADS * X - 1)], block_send)
    drain(pieces, swap_send)
    drain(lroot.at[pl.ds(0, 6 * COLS // X)], pass_send)
    drain(norm.at[0], norm_send)
    drain(adam_in.at[0], adam_send.at[0])
    drain(adam_in.at[pl.ds(0, 3)], adam_send.at[1])
    drain(adam_in.at[pl.ds(0, 3)], adam_send.at[2])
    drain(adam_in.at[pl.ds(0, 7)], adam_send.at[3])
    for k in range(2):
        around = lax.rem(g - 2 * core - k + X, X)
        for steps, blocks in ((0, 8), (1, 5), (2, 2), (3, 5)):

            @pl.when(around == steps)
            def _():
                drain(lroot.at[pl.ds(0, blocks * COLS // X)], root_send.at[k])

        around = lax.rem(2 * core + k - g + X, X)
        for which in range(2):

            @pl.when(lax.rem(around, 2) == 1)
            def _():
                drain(gleft.at[k], gram_send.at[which, k])

            @pl.when(around == 2)
            def _():
                drain(relay, gram_send.at[which, k])

    for which in range(2):
        drain(relay, relay_send.at[which])

    @pl.when(at_home)
    def _():
        drain(pieces.at[pl.ds(0, QUADS * X - 1)], out_send)

    @pl.when(jnp.logical_not(at_home))
    def _():
        drain(pieces, out_send)

    drain(returned, out_recv)

    def one_direction(b, carry):
        directions[b] = returned[slot_ref[b]]
        return carry

    lax.fori_loop(0, NBLK, one_direction, 0, unroll=8)
    store_directions = pltpu.make_async_copy(directions, directions_ref, store_sem.at[5])
    store_directions.start()
    store_directions.wait()

    store_moment.wait()
    for store in store_left + store_right:
        store.wait()


def run_exchange(grads, second_moment, slot_of, block_rows, block_cols, *matrices):
    half = jnp.bfloat16
    away = pl.BlockSpec(memory_space=pl.ANY)
    numbers = pl.BlockSpec(memory_space=pltpu.SMEM)
    dma = pltpu.SemaphoreType.DMA
    operands = (slot_of, block_rows, block_cols, grads, second_moment, *matrices)
    return pl.pallas_call(
        exchange,
        out_shape=(
            pltpu.VMEM((NBLK, ROWS, COLS), half),
            pltpu.VMEM((NBLK, ROWS, COLS), jnp.float32),
            pltpu.VMEM((2, COLS, EDGE), jnp.float32),
            pltpu.VMEM((2, COLS, EDGE), jnp.float32),
        ),
        in_specs=[numbers] * 3 + [away] * 6,
        out_specs=(away, away, away, away),
        scratch_shapes=[
            pltpu.VMEM((QUADS * X, ROWS, COLS), half),
            pltpu.VMEM((NBLK, ROWS, COLS), half),
            pltpu.VMEM((NBLK, ROWS, COLS), jnp.float32),
            pltpu.VMEM((2, COLS, EDGE), jnp.float32),
            pltpu.VMEM((2, COLS, EDGE), jnp.float32),
            pltpu.VMEM((NBLK + 1, ROWS, COLS), half),
            pltpu.VMEM((NBLK, ROWS, COLS), jnp.float32),
            pltpu.VMEM((8, 128), jnp.int32),
            pltpu.SMEM((8, 128), jnp.int32),
            pltpu.VMEM((NBLK, 128), jnp.int32),
            pltpu.VMEM((NBLK, 8, 128), jnp.float32),
            pltpu.VMEM((QUADS * X, ROWS, COLS), half),
            pltpu.VMEM((2, COLS, EDGE), half),
            pltpu.VMEM((2, COLS, EDGE), half),
            pltpu.VMEM((Z, Y, 2, ROWS, EDGE), half),
            pltpu.VMEM((EDGE, EDGE), half),
            pltpu.VMEM((EDGE, EDGE), half),
            pltpu.VMEM((Z, Y, 2, ROWS, HALF), half),
            pltpu.VMEM((EDGE, HALF), jnp.float32),
            pltpu.VMEM((QUADS * 2, ROWS, HALF), half),
            pltpu.VMEM((2, COLS, EDGE), half),
            pltpu.VMEM((2, COLS, EDGE), half),
            pltpu.VMEM((2, COLS, EDGE), jnp.float32),
            pltpu.VMEM((2, COLS, COLS), half),
            pltpu.VMEM((2, 2, COLS, COLS), half),
            pltpu.VMEM((14, 8, 128), jnp.float32),
            pltpu.VMEM((4, 8, 128), jnp.float32),
            pltpu.VMEM((2, 8, 128), jnp.float32),
            dma,
            dma((Y,)),
            dma,
            dma((Y,)),
            dma((2,)),
            dma,
            dma,
            dma,
            dma,
            dma((2, 2)),
            dma((2, 2)),
            dma((2,)),
            dma((2,)),
            dma((4,)),
            dma((4,)),
            dma,
            dma,
            dma,
            dma,
            dma((4,)),
            dma((6,)),
            dma,
        ],
        compiler_params=pltpu.CompilerParams(
            has_side_effects=True, vmem_limit_bytes=48 * 1024 * 1024
        ),
        cost_estimate=pl.CostEstimate(
            flops=8 * EDGE * EDGE * HALF, bytes_accessed=8 * EDGE * EDGE, transcendentals=0
        ),
    )(*[pltpu.with_memory_space_constraint(operand, pltpu.HBM) for operand in operands])


def solution(mesh):
    placed = (
        P(None, "fsdp", "group"),
        P(None, "fsdp", "group"),
        P(),
        P(),
        P(),
        P("fsdp", "group", None),
        P("fsdp", "group", None),
        P("fsdp", "group", None),
        P("fsdp", None, "group"),
    )
    return jax.shard_map(
        run_exchange,
        mesh=mesh,
        in_specs=placed,
        out_specs=(
            P(None, "fsdp", "group"),
            P(None, "fsdp", "group"),
            P("fsdp", "group", None),
            P("fsdp", "group", None),
        ),
        check_vma=False,
    )
```

```python
import jax
import jax.numpy as jnp
from jax import lax
from jax.experimental import pallas as pl
from jax.experimental.pallas import tpu as pltpu
from jax.sharding import PartitionSpec as P

MESH = pl.DeviceIdType.MESH
Z, Y, X = 8, 4, 4
QUADS = Z * Y
EDGE = 1024
NBLK = 56
HALF = EDGE // 2
ROWS, COLS = 16, 256
FAR_FIRST = (4, 3, 5, 2, 6, 1, 7, 0)


def drain(ref, sem):
    pltpu.make_async_copy(ref, ref, sem).wait()


def exchange(
    slot_ref,
    rows_ref,
    cols_ref,
    grads_ref,
    second_ref,
    lstat_ref,
    rstat_ref,
    lroot_ref,
    rroot_ref,
    directions_ref,
    moment_ref,
    new_left_ref,
    new_right_ref,
    returned,
    directions,
    moments,
    new_left,
    new_right,
    grads,
    second,
    table,
    table_smem,
    matches,
    adam_parts,
    pieces,
    gleft_in,
    gright_in,
    block,
    lroot,
    rroot,
    mixed,
    precond,
    direction,
    gleft,
    gright,
    gram_part,
    relay,
    cross,
    adam_in,
    adam_sum,
    norm,
    block_send,
    block_recv,
    swap_send,
    swap_recv,
    root_send,
    root_recv,
    row_recv,
    pass_send,
    pass_recv,
    gram_send,
    gram_recv,
    relay_send,
    relay_recv,
    adam_send,
    adam_recv,
    norm_send,
    norm_recv,
    out_send,
    out_recv,
    load_sem,
    store_sem,
    table_sem,
):
    f = lax.axis_index("fsdp")
    g = lax.axis_index("group")
    core = lax.rem(f, 2)
    quad = lax.div(f, 2)
    y = lax.rem(quad, Y)
    z = lax.div(quad, Y)
    slot = quad * X + g
    other = f + 1 - 2 * core
    side = lax.div(g, 2)
    parity = lax.rem(g, 2)
    at_home = side == core

    def device(zz, yy, cc):
        return (zz * Y + yy) * 2 + cc

    def remote(src, dst, send, recv, ff, gg):
        pltpu.make_async_remote_copy(
            src_ref=src,
            dst_ref=dst,
            send_sem=send,
            recv_sem=recv,
            device_id=(ff, gg),
            device_id_type=MESH,
        ).start()

    def span(j):
        return pl.ds(pl.multiple_of(lax.rem(j, X) * COLS, COLS), COLS)

    def left_block(ref, j, k):
        return ref.at[span(j), span(k)]

    def send_root(k, ff, xx, lefts, rights):
        for d in lefts:
            src = lroot_ref.at[k, :, span(g + d)]
            remote(src, left_block(lroot, g, g + d), root_send.at[k], root_recv, ff, xx)
        for d in rights:
            src = rroot_ref.at[k, span(g + d), :]
            remote(src, left_block(rroot, g + d, g), root_send.at[k], root_recv, ff, xx)

    def send_roots():
        for k in range(2):
            home = 2 * core + k
            around = lax.rem(g - home + X, X)

            @pl.when(around == 0)
            def _():
                for src, dst in ((lroot_ref.at[k], lroot.at[span(g)]), (rroot_ref.at[k], rroot.at[:, span(g)])):
                    remote(src, dst, root_send.at[k], row_recv, other, g)
                    pltpu.make_async_copy(src, dst, row_recv).start()

            @pl.when(around == 1)
            def _():
                send_root(k, quad * 2, home, (0, 1, 2), (0, 1))

            @pl.when(around == 2)
            def _():
                send_root(k, quad * 2, home, (0,), ())
                send_root(k, quad * 2 + 1, home, (), (0,))

            @pl.when(around == 3)
            def _():
                send_root(k, quad * 2 + 1, home, (0, 3), (0, 3, 2))

    load_grads = pltpu.make_async_copy(grads_ref, grads.at[pl.ds(0, NBLK)], load_sem.at[0])
    load_second = pltpu.make_async_copy(second_ref, second, load_sem.at[1])
    load_left = pltpu.make_async_copy(lstat_ref, new_left, load_sem.at[2])
    load_right = pltpu.make_async_copy(rstat_ref, new_right, load_sem.at[3])
    load_grads.start()
    load_second.start()
    barrier = pltpu.get_barrier_semaphore()

    def greet(ff, gg):
        pl.semaphore_signal(barrier, inc=1, device_id=(ff, gg), device_id_type=MESH)

    for d in range(X):
        greet(other, lax.rem(g + d, X))
        if d:
            greet(f, lax.rem(g + d, X))

    @pl.loop(1, QUADS)
    def _(n):
        for d in range(X):
            greet(lax.rem(quad + n, QUADS) * 2 + core, lax.rem(g + d, X))

    lane = lax.broadcasted_iota(jnp.int32, (8, 128), 1)

    def valid(b):
        return (f * ROWS < rows_ref[b]) & (g * COLS < cols_ref[b])

    source = jnp.full((8, 128), NBLK, jnp.int32)
    for b in range(NBLK):
        match = lane == slot_ref[b]
        source = jnp.where(match, jnp.where(valid(b), b, NBLK), source)
        matches[pl.ds(b, 1)] = match[0:1].astype(jnp.int32)
    table[...] = source
    to_smem = pltpu.make_async_copy(table, table_smem, table_sem)
    to_smem.start()
    grads[NBLK] = jnp.zeros((ROWS, COLS), jnp.bfloat16)
    to_smem.wait()
    load_grads.wait()

    mine = block.at[z, y, core, :, pl.ds(pl.multiple_of(g * COLS, COLS), COLS)]

    @pl.loop(0, QUADS * X // 8)
    def _(n):
        for k in range(8):
            pieces[n * 8 + k] = grads[table_smem[0, n * 8 + k]]

    pl.semaphore_wait(barrier, QUADS * X + 3)
    send_roots()

    def send_blocks(step, carry):
        dy, dx = lax.div(step, X), lax.rem(step, X)
        yy, xx = lax.rem(y + dy, Y), lax.rem(g + dx, X)
        for dz in FAR_FIRST:
            zz = lax.rem(z + dz, Z)
            at = (zz * Y + yy) * X + xx
            src = pieces.at[at]
            if dz:
                remote(src, mine, block_send, block_recv.at[dy], device(zz, yy, core), xx)
            else:

                @pl.when(step == 0)
                def _():
                    pltpu.make_async_copy(src, mine, block_recv.at[0]).start()

                @pl.when(step != 0)
                def _():
                    remote(src, mine, block_send, block_recv.at[dy], device(zz, yy, core), xx)

        return carry

    lax.fori_loop(0, X * Y, send_blocks, 0)

    load_left.start()
    load_right.start()

    load_second.wait()

    def one_block(b, carry):
        grad = jnp.where(valid(b), grads[b].astype(jnp.float32), 0.0)
        moment = 0.95 * second[b] + 0.05 * grad * grad
        moments[b] = moment
        adam = grad / (jnp.sqrt(moment) + 1e-08)
        adam = adam * adam
        adam = adam[0:8] + adam[8:16]
        adam_parts[b] = adam[:, 0:128] + adam[:, 128:256]
        return carry

    lax.fori_loop(0, NBLK, one_block, 0, unroll=4)
    adam = jnp.sum(jnp.sum(adam_parts[...], axis=1), axis=1, keepdims=True)
    adam = jnp.where(matches[...] != 0, adam, 0.0)
    adam_sum[0] = jnp.broadcast_to(jnp.sum(adam, axis=0, keepdims=True), (8, 128))
    store_moment = pltpu.make_async_copy(moments, moment_ref, store_sem.at[0])
    store_moment.start()

    def adam_stage(stage, first, peers):
        for d, (ff, gg) in enumerate(peers):
            remote(adam_sum.at[stage], adam_in.at[first + d], adam_send.at[stage], adam_recv.at[stage], ff, gg)

    def adam_add(stage, first, count):
        drain(adam_in.at[pl.ds(first, count)], adam_recv.at[stage])
        total = adam_sum[stage]
        for d in range(count):
            total = total + adam_in[first + d]
        return total

    adam_stage(0, 0, [(other, g)])

    def pass_on(ref, j, k):
        here = left_block(ref, j, k)
        remote(here, here, pass_send, pass_recv, other, g)

    drain(lroot.at[pl.ds(0, 6 * COLS // X)], root_recv)

    @pl.when(core == 0)
    def _():
        for ref, j, k in ((lroot, 1, 1), (lroot, 1, 2), (lroot, 1, 3), (lroot, 2, 2), (rroot, 1, 1), (rroot, 2, 1)):
            pass_on(ref, g + j, g + k)

    @pl.when(core == 1)
    def _():
        for ref, j, k in ((lroot, 3, 3), (lroot, 3, 2), (rroot, 3, 3), (rroot, 2, 3), (rroot, 1, 3), (rroot, 2, 2)):
            pass_on(ref, g + j, g + k)

    adam_sum[1] = adam_add(0, 0, 1)
    adam_stage(1, 1, [(f, lax.rem(g + d, X)) for d in range(1, X)])

    drain(lroot.at[pl.ds(0, 2 * COLS)], row_recv)
    drain(lroot.at[pl.ds(0, 6 * COLS // X)], pass_recv)
    for j, k in ((1, 0), (2, 0), (3, 0), (2, 1), (2, 3), (1, 3)):
        rroot[span(g + k), span(g + j)] = rroot[span(g + j), span(g + k)].T
    for j, k in ((0, 1), (0, 2), (0, 3), (1, 2), (3, 2), (1, 3)):
        lroot[span(g + k), span(g + j)] = lroot[span(g + j), span(g + k)].T
    half = pl.ds(pl.multiple_of(core * HALF, HALF), HALF)

    def send_gram(which, m, src, dst):
        xx = 2 * core + m
        ff = quad * 2 + side
        around = lax.rem(xx - g + X, X)
        send = gram_send.at[which, m]

        @pl.when(around == 0)
        def _():
            pltpu.make_async_copy(src.at[m], dst.at[parity], gram_recv.at[which, parity]).start()

        @pl.when(lax.rem(around, 2) == 1)
        def _():
            remote(src.at[m], dst.at[parity], send, gram_recv.at[which, parity], ff, xx)

        @pl.when(around == 2)
        def _():
            for d, gg in ((0, lax.rem(g + 1, X)), (2, lax.rem(g + 3, X))):
                remote(src.at[m, :, span(g + d)], relay.at[which], send, relay_recv.at[which], ff, gg)

    def swap(d):
        ys = lax.rem(y + Y - d, Y)
        rows = block.at[:, ys, core]
        drain(rows, block_recv.at[d])
        remote(rows, rows, swap_send, swap_recv.at[d], other, g)

    def group(d):
        ys = lax.rem(y + Y - d, Y)
        drain(block.at[:, ys, 1 - core], swap_recv.at[d])
        for m in range(2):
            at = pl.multiple_of(core * HALF + m * COLS, COLS)
            value = lax.dot_general(
                block[:, ys, :, :, pl.ds(at, COLS)].reshape(COLS, COLS),
                block[:, ys].reshape(COLS, EDGE),
                (((0,), (0,)), ((), ())),
                preferred_element_type=jnp.float32,
            )
            if d:
                value = gram_part[m] + value
            if d < Y - 1:
                gram_part[m] = value
            else:
                gright[m] = value.astype(jnp.bfloat16)
                send_gram(1, m, gright, gright_in)
        value = jnp.dot(
            block[:, ys].reshape(COLS, EDGE), rroot[:, half], preferred_element_type=jnp.float32
        )
        mixed[:, ys] = value.astype(jnp.bfloat16).reshape(Z, 2, ROWS, HALF)

    swap(0)
    swap(1)
    group(0)
    swap(2)
    group(1)
    swap(3)
    group(2)
    group(3)

    adam_sum[2] = adam_add(1, 1, X - 1)
    adam_stage(2, 4, [(device(z, lax.rem(y + d, Y), core), g) for d in range(1, Y)])

    rows_valid, cols_valid = 0, 0
    for b in range(NBLK):
        rows_valid = jnp.where(slot_ref[b] == slot, rows_ref[b], rows_valid)
        cols_valid = jnp.where(slot_ref[b] == slot, cols_ref[b], cols_valid)
    cols_keep = (core * HALF + lax.broadcasted_iota(jnp.int32, (COLS, HALF), 1)) < cols_valid

    def one_part(m, total):
        at = pl.multiple_of(m * COLS, COLS)
        value = jnp.dot(lroot[pl.ds(at, COLS)], mixed[...].reshape(EDGE, HALF), preferred_element_type=jnp.float32)
        rows_keep = (at + lax.broadcasted_iota(jnp.int32, (COLS, HALF), 0)) < rows_valid
        value = jnp.where(rows_keep & cols_keep, value, 0.0)
        precond[pl.ds(at, COLS)] = value
        square = value * value
        return total + jnp.sum(square.reshape(COLS // 8, 8, HALF), axis=0)

    total = lax.fori_loop(0, 4, one_part, jnp.zeros((8, HALF), jnp.float32))
    norm[0] = jnp.broadcast_to(jnp.sum(total, keepdims=True), (8, 128))
    remote(norm.at[0], norm.at[1], norm_send, norm_recv, other, g)

    adam_sum[3] = adam_add(2, 4, Y - 1)
    adam_stage(3, 7, [(device(lax.rem(z + d, Z), y, core), g) for d in range(1, Z)])

    for m in range(2):
        gleft[m] = lax.dot_general(
            block[pl.ds(core * 4 + m * 2, 2)].reshape(COLS, EDGE),
            block[...].reshape(EDGE, EDGE),
            (((1,), (1,)), ((), ())),
            preferred_element_type=jnp.float32,
        ).astype(jnp.bfloat16)
        send_gram(0, m, gleft, gleft_in)

    adam = adam_add(3, 7, Z - 1)
    adam = jnp.sum(jnp.where(lane == slot, adam, 0.0)[0:1], keepdims=True)

    drain(norm.at[1], norm_recv)
    squares = (norm[0] + norm[1])[0:1, 0:1]
    factor = jnp.sqrt(adam) / (jnp.sqrt(squares) + 1e-06)

    @pl.loop(0, 4)
    def _(m):
        at = pl.multiple_of(m * COLS, COLS)
        value = (precond[pl.ds(at, COLS)] * factor).astype(jnp.bfloat16)
        direction[pl.ds(m * 16, 16)] = value.reshape(16, ROWS, HALF)

    def send_out(step, carry):
        dy, dc, e = lax.div(step, 4), lax.rem(lax.div(step, 2), 2), lax.rem(step, 2)
        yy, cc, xx = lax.rem(y + dy, Y), lax.rem(core + dc, 2), 2 * core + e
        for dz in FAR_FIRST:
            ff = device(lax.rem(z + dz, Z), yy, cc)
            src = direction.at[ff, :, pl.ds(pl.multiple_of(e * COLS, COLS), COLS)]
            dst = returned.at[slot]
            if dz:
                remote(src, dst, out_send, out_recv, ff, xx)
            else:
                local = (step < 2) & at_home & (parity == e)

                @pl.when(local)
                def _():
                    pltpu.make_async_copy(src, dst, out_recv).start()

                @pl.when(jnp.logical_not(local))
                def _():
                    remote(src, dst, out_send, out_recv, ff, xx)

        return carry

    lax.fori_loop(0, 16, send_out, 0)

    arounds = [lax.rem(g - 2 * core - k + X, X) for k in range(2)]
    for which, gram in ((1, gright_in), (0, gleft_in)):
        for k in range(2):
            for way in (1, 3):

                @pl.when(arounds[k] == way)
                def _():
                    drain(gram.at[k], gram_recv.at[which, k])
                    drain(relay.at[which], relay_recv.at[which])
                    gg = lax.rem(g + way, X)
                    here = gram.at[k, :, span(g + way)]
                    send = relay_send.at[which]
                    recv = gram_recv.at[which, k]
                    remote(here, cross.at[which, way // 2], send, recv, f, gg)
                    column = span(g + 3)
                    remote(relay.at[which], gram.at[k, :, column], send, recv, f, gg)

    def update(target, gram, k):
        @pl.loop(0, 8)
        def _(m):
            at = pl.ds(pl.multiple_of(m * 32, 32), 32)
            target[k, at] = 0.9 * target[k, at] + 0.1 * gram[k, at].astype(jnp.float32)

    store_left = [pltpu.make_async_copy(new_left.at[k], new_left_ref.at[k], store_sem.at[1 + k]) for k in range(2)]
    store_right = [pltpu.make_async_copy(new_right.at[k], new_right_ref.at[k], store_sem.at[3 + k]) for k in range(2)]
    parts = ((1, new_right, gright_in, store_right), (0, new_left, gleft_in, store_left))
    load_left.wait()
    load_right.wait()
    for last in (False, True):
        for which, target, gram, store in parts:
            for k in range(2):

                @pl.when((arounds[k] == 2) == last)
                def _():
                    if last:
                        drain(gram.at[k], gram_recv.at[which, k])
                        gram[k, :, span(g + 3)] = cross[which, 0].T
                        gram[k, :, span(g + 1)] = cross[which, 1].T
                    else:

                        @pl.when(arounds[k] == 0)
                        def _():
                            drain(gram.at[k], gram_recv.at[which, k])

                    update(target, gram, k)
                    store[k].start()

    drain(pieces.at[pl.ds(0, QUADS * X - 1)], block_send)
    drain(pieces, swap_send)
    drain(lroot.at[pl.ds(0, 6 * COLS // X)], pass_send)
    drain(norm.at[0], norm_send)
    drain(adam_in.at[0], adam_send.at[0])
    drain(adam_in.at[pl.ds(0, 3)], adam_send.at[1])
    drain(adam_in.at[pl.ds(0, 3)], adam_send.at[2])
    drain(adam_in.at[pl.ds(0, 7)], adam_send.at[3])
    for k in range(2):
        around = lax.rem(g - 2 * core - k + X, X)
        for steps, blocks in ((0, 8), (1, 5), (2, 2), (3, 5)):

            @pl.when(around == steps)
            def _():
                drain(lroot.at[pl.ds(0, blocks * COLS // X)], root_send.at[k])

        around = lax.rem(2 * core + k - g + X, X)
        for which in range(2):

            @pl.when(lax.rem(around, 2) == 1)
            def _():
                drain(gleft.at[k], gram_send.at[which, k])

            @pl.when(around == 2)
            def _():
                drain(relay, gram_send.at[which, k])

    for which in range(2):
        drain(relay, relay_send.at[which])

    @pl.when(at_home)
    def _():
        drain(pieces.at[pl.ds(0, QUADS * X - 1)], out_send)

    @pl.when(jnp.logical_not(at_home))
    def _():
        drain(pieces, out_send)

    drain(returned, out_recv)

    def one_direction(b, carry):
        directions[b] = returned[slot_ref[b]]
        return carry

    lax.fori_loop(0, NBLK, one_direction, 0, unroll=8)
    store_directions = pltpu.make_async_copy(directions, directions_ref, store_sem.at[5])
    store_directions.start()
    store_directions.wait()

    store_moment.wait()
    for store in store_left + store_right:
        store.wait()


def run_exchange(grads, second_moment, slot_of, block_rows, block_cols, *matrices):
    half = jnp.bfloat16
    away = pl.BlockSpec(memory_space=pl.ANY)
    numbers = pl.BlockSpec(memory_space=pltpu.SMEM)
    dma = pltpu.SemaphoreType.DMA
    operands = (slot_of, block_rows, block_cols, grads, second_moment, *matrices)
    return pl.pallas_call(
        exchange,
        out_shape=(
            pltpu.VMEM((NBLK, ROWS, COLS), half),
            pltpu.VMEM((NBLK, ROWS, COLS), jnp.float32),
            pltpu.VMEM((2, COLS, EDGE), jnp.float32),
            pltpu.VMEM((2, COLS, EDGE), jnp.float32),
        ),
        in_specs=[numbers] * 3 + [away] * 6,
        out_specs=(away, away, away, away),
        scratch_shapes=[
            pltpu.VMEM((QUADS * X, ROWS, COLS), half),
            pltpu.VMEM((NBLK, ROWS, COLS), half),
            pltpu.VMEM((NBLK, ROWS, COLS), jnp.float32),
            pltpu.VMEM((2, COLS, EDGE), jnp.float32),
            pltpu.VMEM((2, COLS, EDGE), jnp.float32),
            pltpu.VMEM((NBLK + 1, ROWS, COLS), half),
            pltpu.VMEM((NBLK, ROWS, COLS), jnp.float32),
            pltpu.VMEM((8, 128), jnp.int32),
            pltpu.SMEM((8, 128), jnp.int32),
            pltpu.VMEM((NBLK, 128), jnp.int32),
            pltpu.VMEM((NBLK, 8, 128), jnp.float32),
            pltpu.VMEM((QUADS * X, ROWS, COLS), half),
            pltpu.VMEM((2, COLS, EDGE), half),
            pltpu.VMEM((2, COLS, EDGE), half),
            pltpu.VMEM((Z, Y, 2, ROWS, EDGE), half),
            pltpu.VMEM((EDGE, EDGE), half),
            pltpu.VMEM((EDGE, EDGE), half),
            pltpu.VMEM((Z, Y, 2, ROWS, HALF), half),
            pltpu.VMEM((EDGE, HALF), jnp.float32),
            pltpu.VMEM((QUADS * 2, ROWS, HALF), half),
            pltpu.VMEM((2, COLS, EDGE), half),
            pltpu.VMEM((2, COLS, EDGE), half),
            pltpu.VMEM((2, COLS, EDGE), jnp.float32),
            pltpu.VMEM((2, COLS, COLS), half),
            pltpu.VMEM((2, 2, COLS, COLS), half),
            pltpu.VMEM((14, 8, 128), jnp.float32),
            pltpu.VMEM((4, 8, 128), jnp.float32),
            pltpu.VMEM((2, 8, 128), jnp.float32),
            dma,
            dma((Y,)),
            dma,
            dma((Y,)),
            dma((2,)),
            dma,
            dma,
            dma,
            dma,
            dma((2, 2)),
            dma((2, 2)),
            dma((2,)),
            dma((2,)),
            dma((4,)),
            dma((4,)),
            dma,
            dma,
            dma,
            dma,
            dma((4,)),
            dma((6,)),
            dma,
        ],
        compiler_params=pltpu.CompilerParams(
            collective_id=0, has_side_effects=True, vmem_limit_bytes=48 * 1024 * 1024
        ),
        cost_estimate=pl.CostEstimate(
            flops=8 * EDGE * EDGE * HALF, bytes_accessed=8 * EDGE * EDGE, transcendentals=0
        ),
    )(*[pltpu.with_memory_space_constraint(operand, pltpu.HBM) for operand in operands])


def solution(mesh):
    placed = (
        P(None, "fsdp", "group"),
        P(None, "fsdp", "group"),
        P(),
        P(),
        P(),
        P("fsdp", "group", None),
        P("fsdp", "group", None),
        P("fsdp", "group", None),
        P("fsdp", None, "group"),
    )
    return jax.shard_map(
        run_exchange,
        mesh=mesh,
        in_specs=placed,
        out_specs=(
            P(None, "fsdp", "group"),
            P(None, "fsdp", "group"),
            P("fsdp", "group", None),
            P("fsdp", "group", None),
        ),
        check_vma=False,
    )
```

```python
import jax
import jax.numpy as jnp
from jax import lax
from jax.experimental import pallas as pl
from jax.experimental.pallas import tpu as pltpu
from jax.sharding import PartitionSpec as P

MESH = pl.DeviceIdType.MESH
Z, Y, X = 8, 4, 4
QUADS = Z * Y
EDGE = 1024
NBLK = 56
HALF = EDGE // 2
ROWS, COLS = 16, 256
FAR_FIRST = (4, 3, 5, 2, 6, 1, 7, 0)


def drain(ref, sem):
    pltpu.make_async_copy(ref, ref, sem).wait()


def exchange(
    slot_ref,
    rows_ref,
    cols_ref,
    grads_ref,
    second_ref,
    lstat_ref,
    rstat_ref,
    lroot_ref,
    rroot_ref,
    directions,
    moments,
    new_left,
    new_right,
    returned,
    grads,
    second,
    table,
    table_smem,
    matches,
    adam_parts,
    pieces,
    gleft_in,
    gright_in,
    block,
    lroot,
    rroot,
    mixed,
    precond,
    direction,
    gleft,
    gright,
    gram_part,
    relay,
    cross,
    adam_in,
    adam_sum,
    norm,
    block_send,
    block_recv,
    swap_send,
    swap_recv,
    root_send,
    root_recv,
    row_recv,
    pass_send,
    pass_recv,
    gram_send,
    gram_recv,
    relay_send,
    relay_recv,
    adam_send,
    adam_recv,
    norm_send,
    norm_recv,
    out_send,
    out_recv,
    load_sem,
    table_sem,
    ready,
):
    f = lax.axis_index("fsdp")
    g = lax.axis_index("group")
    core = lax.rem(f, 2)
    quad = lax.div(f, 2)
    y = lax.rem(quad, Y)
    z = lax.div(quad, Y)
    slot = quad * X + g
    other = f + 1 - 2 * core
    side = lax.div(g, 2)
    parity = lax.rem(g, 2)
    at_home = side == core

    def device(zz, yy, cc):
        return (zz * Y + yy) * 2 + cc

    def remote(src, dst, send, recv, ff, gg):
        pltpu.make_async_remote_copy(
            src_ref=src,
            dst_ref=dst,
            send_sem=send,
            recv_sem=recv,
            device_id=(ff, gg),
            device_id_type=MESH,
        ).start()

    def span(j):
        return pl.ds(pl.multiple_of(lax.rem(j, X) * COLS, COLS), COLS)

    def left_block(ref, j, k):
        return ref.at[span(j), span(k)]

    def send_root(k, ff, xx, lefts, rights):
        for d in lefts:
            src = lroot_ref.at[k, :, span(g + d)]
            remote(src, left_block(lroot, g, g + d), root_send.at[k], root_recv, ff, xx)
        for d in rights:
            src = rroot_ref.at[k, span(g + d), :]
            remote(src, left_block(rroot, g + d, g), root_send.at[k], root_recv, ff, xx)

    def send_roots():
        for k in range(2):
            home = 2 * core + k
            around = lax.rem(g - home + X, X)

            @pl.when(around == 0)
            def _():
                for src, dst in ((lroot_ref.at[k], lroot.at[span(g)]), (rroot_ref.at[k], rroot.at[:, span(g)])):
                    remote(src, dst, root_send.at[k], row_recv, other, g)
                    pltpu.make_async_copy(src, dst, row_recv).start()

            @pl.when(around == 1)
            def _():
                send_root(k, quad * 2, home, (0, 1, 2), (0, 1))

            @pl.when(around == 2)
            def _():
                send_root(k, quad * 2, home, (0,), ())
                send_root(k, quad * 2 + 1, home, (), (0,))

            @pl.when(around == 3)
            def _():
                send_root(k, quad * 2 + 1, home, (0, 3), (0, 3, 2))

    load_grads = pltpu.make_async_copy(grads_ref, grads.at[pl.ds(0, NBLK)], load_sem.at[0])
    load_second = pltpu.make_async_copy(second_ref, second, load_sem.at[1])
    load_left = pltpu.make_async_copy(lstat_ref, new_left, load_sem.at[2])
    load_right = pltpu.make_async_copy(rstat_ref, new_right, load_sem.at[3])
    load_grads.start()
    load_second.start()
    barrier = pltpu.get_barrier_semaphore()
    along_z = [device(lax.rem(z + d, Z), y, core) for d in range(1, Z)]

    def greet(sem, ff, gg):
        pl.semaphore_signal(sem, inc=1, device_id=(ff, gg), device_id_type=MESH)

    for ff in along_z:
        greet(barrier, ff, g)
    for dx in range(X):
        greet(barrier, other, lax.rem(g + dx, X))
        for dy in range(Y):
            if dx or dy:
                greet(barrier, device(z, lax.rem(y + dy, Y), core), lax.rem(g + dx, X))

    lane = lax.broadcasted_iota(jnp.int32, (8, 128), 1)

    def valid(b):
        return (f * ROWS < rows_ref[b]) & (g * COLS < cols_ref[b])

    source = jnp.full((8, 128), NBLK, jnp.int32)
    for b in range(NBLK):
        match = lane == slot_ref[b]
        source = jnp.where(match, jnp.where(valid(b), b, NBLK), source)
        matches[pl.ds(b, 1)] = match[0:1].astype(jnp.int32)
    table[...] = source
    to_smem = pltpu.make_async_copy(table, table_smem, table_sem)
    to_smem.start()
    grads[NBLK] = jnp.zeros((ROWS, COLS), jnp.bfloat16)
    pl.semaphore_wait(barrier, X * Y - 1 + Z - 1 + X)
    for ff in along_z:
        greet(ready, ff, g)
    send_roots()
    to_smem.wait()
    load_grads.wait()

    mine = block.at[z, y, core, :, pl.ds(pl.multiple_of(g * COLS, COLS), COLS)]

    @pl.loop(0, QUADS * X // 8)
    def _(n):
        for k in range(8):
            pieces[n * 8 + k] = grads[table_smem[0, n * 8 + k]]

    pl.semaphore_wait(ready, Z - 1)

    def send_blocks(step, carry):
        dy, dx = lax.div(step, X), lax.rem(step, X)
        yy, xx = lax.rem(y + dy, Y), lax.rem(g + dx, X)
        for dz in FAR_FIRST:
            zz = lax.rem(z + dz, Z)
            at = (zz * Y + yy) * X + xx
            src = pieces.at[at]
            if dz:
                remote(src, mine, block_send, block_recv.at[dy], device(zz, yy, core), xx)
            else:

                @pl.when(step == 0)
                def _():
                    pltpu.make_async_copy(src, mine, block_recv.at[0]).start()

                @pl.when(step != 0)
                def _():
                    remote(src, mine, block_send, block_recv.at[dy], device(zz, yy, core), xx)

        return carry

    lax.fori_loop(0, X * Y, send_blocks, 0)

    load_left.start()
    load_right.start()

    load_second.wait()

    def one_block(b, carry):
        grad = jnp.where(valid(b), grads[b].astype(jnp.float32), 0.0)
        moment = 0.95 * second[b] + 0.05 * grad * grad
        moments[b] = moment
        adam = grad / (jnp.sqrt(moment) + 1e-08)
        adam = adam * adam
        adam = adam[0:8] + adam[8:16]
        adam_parts[b] = adam[:, 0:128] + adam[:, 128:256]
        return carry

    lax.fori_loop(0, NBLK, one_block, 0, unroll=4)
    adam = jnp.sum(jnp.sum(adam_parts[...], axis=1), axis=1, keepdims=True)
    adam = jnp.where(matches[...] != 0, adam, 0.0)
    adam_sum[0] = jnp.broadcast_to(jnp.sum(adam, axis=0, keepdims=True), (8, 128))

    def adam_stage(stage, first, peers):
        for d, (ff, gg) in enumerate(peers):
            remote(adam_sum.at[stage], adam_in.at[first + d], adam_send.at[stage], adam_recv.at[stage], ff, gg)

    def adam_add(stage, first, count):
        drain(adam_in.at[pl.ds(first, count)], adam_recv.at[stage])
        total = adam_sum[stage]
        for d in range(count):
            total = total + adam_in[first + d]
        return total

    adam_stage(0, 0, [(other, g)])

    def pass_on(ref, j, k):
        here = left_block(ref, j, k)
        remote(here, here, pass_send, pass_recv, other, g)

    drain(lroot.at[pl.ds(0, 6 * COLS // X)], root_recv)

    @pl.when(core == 0)
    def _():
        for ref, j, k in ((lroot, 1, 1), (lroot, 1, 2), (lroot, 1, 3), (lroot, 2, 2), (rroot, 1, 1), (rroot, 2, 1)):
            pass_on(ref, g + j, g + k)

    @pl.when(core == 1)
    def _():
        for ref, j, k in ((lroot, 3, 3), (lroot, 3, 2), (rroot, 3, 3), (rroot, 2, 3), (rroot, 1, 3), (rroot, 2, 2)):
            pass_on(ref, g + j, g + k)

    adam_sum[1] = adam_add(0, 0, 1)
    adam_stage(1, 1, [(f, lax.rem(g + d, X)) for d in range(1, X)])

    drain(lroot.at[pl.ds(0, 2 * COLS)], row_recv)
    drain(lroot.at[pl.ds(0, 6 * COLS // X)], pass_recv)
    for j, k in ((1, 0), (2, 0), (3, 0), (2, 1), (2, 3), (1, 3)):
        rroot[span(g + k), span(g + j)] = rroot[span(g + j), span(g + k)].T
    for j, k in ((0, 1), (0, 2), (0, 3), (1, 2), (3, 2), (1, 3)):
        lroot[span(g + k), span(g + j)] = lroot[span(g + j), span(g + k)].T
    half = pl.ds(pl.multiple_of(core * HALF, HALF), HALF)

    def send_gram(which, m, src, dst):
        xx = 2 * core + m
        ff = quad * 2 + side
        around = lax.rem(xx - g + X, X)
        send = gram_send.at[which, m]

        @pl.when(around == 0)
        def _():
            pltpu.make_async_copy(src.at[m], dst.at[parity], gram_recv.at[which, parity]).start()

        @pl.when(lax.rem(around, 2) == 1)
        def _():
            remote(src.at[m], dst.at[parity], send, gram_recv.at[which, parity], ff, xx)

        @pl.when(around == 2)
        def _():
            for d, gg in ((0, lax.rem(g + 1, X)), (2, lax.rem(g + 3, X))):
                remote(src.at[m, :, span(g + d)], relay.at[which], send, relay_recv.at[which], ff, gg)

    def swap(d):
        ys = lax.rem(y + Y - d, Y)
        rows = block.at[:, ys, core]
        drain(rows, block_recv.at[d])
        remote(rows, rows, swap_send, swap_recv.at[d], other, g)

    def group(d):
        ys = lax.rem(y + Y - d, Y)
        drain(block.at[:, ys, 1 - core], swap_recv.at[d])
        for m in range(2):
            at = pl.multiple_of(core * HALF + m * COLS, COLS)
            value = lax.dot_general(
                block[:, ys, :, :, pl.ds(at, COLS)].reshape(COLS, COLS),
                block[:, ys].reshape(COLS, EDGE),
                (((0,), (0,)), ((), ())),
                preferred_element_type=jnp.float32,
            )
            if d:
                value = gram_part[m] + value
            if d < Y - 1:
                gram_part[m] = value
            else:
                gright[m] = value.astype(jnp.bfloat16)
                send_gram(1, m, gright, gright_in)
        value = jnp.dot(
            block[:, ys].reshape(COLS, EDGE), rroot[:, half], preferred_element_type=jnp.float32
        )
        mixed[:, ys] = value.astype(jnp.bfloat16).reshape(Z, 2, ROWS, HALF)

    swap(0)
    swap(1)
    group(0)
    swap(2)
    group(1)
    swap(3)
    group(2)
    group(3)

    adam_sum[2] = adam_add(1, 1, X - 1)
    adam_stage(2, 4, [(device(z, lax.rem(y + d, Y), core), g) for d in range(1, Y)])

    rows_valid, cols_valid = 0, 0
    for b in range(NBLK):
        rows_valid = jnp.where(slot_ref[b] == slot, rows_ref[b], rows_valid)
        cols_valid = jnp.where(slot_ref[b] == slot, cols_ref[b], cols_valid)
    cols_keep = (core * HALF + lax.broadcasted_iota(jnp.int32, (COLS, HALF), 1)) < cols_valid

    def one_part(m, total):
        at = pl.multiple_of(m * COLS, COLS)
        value = jnp.dot(lroot[pl.ds(at, COLS)], mixed[...].reshape(EDGE, HALF), preferred_element_type=jnp.float32)
        rows_keep = (at + lax.broadcasted_iota(jnp.int32, (COLS, HALF), 0)) < rows_valid
        value = jnp.where(rows_keep & cols_keep, value, 0.0)
        precond[pl.ds(at, COLS)] = value
        square = value * value
        return total + jnp.sum(square.reshape(COLS // 8, 8, HALF), axis=0)

    total = lax.fori_loop(0, 4, one_part, jnp.zeros((8, HALF), jnp.float32))
    norm[0] = jnp.broadcast_to(jnp.sum(total, keepdims=True), (8, 128))
    remote(norm.at[0], norm.at[1], norm_send, norm_recv, other, g)

    adam_sum[3] = adam_add(2, 4, Y - 1)
    adam_stage(3, 7, [(device(lax.rem(z + d, Z), y, core), g) for d in range(1, Z)])

    for m in range(2):
        gleft[m] = lax.dot_general(
            block[pl.ds(core * 4 + m * 2, 2)].reshape(COLS, EDGE),
            block[...].reshape(EDGE, EDGE),
            (((1,), (1,)), ((), ())),
            preferred_element_type=jnp.float32,
        ).astype(jnp.bfloat16)
        send_gram(0, m, gleft, gleft_in)

    adam = adam_add(3, 7, Z - 1)
    adam = jnp.sum(jnp.where(lane == slot, adam, 0.0)[0:1], keepdims=True)

    drain(norm.at[1], norm_recv)
    squares = (norm[0] + norm[1])[0:1, 0:1]
    factor = jnp.sqrt(adam) / (jnp.sqrt(squares) + 1e-06)

    @pl.loop(0, 4)
    def _(m):
        at = pl.multiple_of(m * COLS, COLS)
        value = (precond[pl.ds(at, COLS)] * factor).astype(jnp.bfloat16)
        direction[pl.ds(m * 16, 16)] = value.reshape(16, ROWS, HALF)

    def send_out(step, carry):
        dy, dc, e = lax.div(step, 4), lax.rem(lax.div(step, 2), 2), lax.rem(step, 2)
        yy, cc, xx = lax.rem(y + dy, Y), lax.rem(core + dc, 2), 2 * core + e
        for dz in FAR_FIRST:
            ff = device(lax.rem(z + dz, Z), yy, cc)
            src = direction.at[ff, :, pl.ds(pl.multiple_of(e * COLS, COLS), COLS)]
            dst = returned.at[slot]
            if dz:
                remote(src, dst, out_send, out_recv, ff, xx)
            else:
                local = (step < 2) & at_home & (parity == e)

                @pl.when(local)
                def _():
                    pltpu.make_async_copy(src, dst, out_recv).start()

                @pl.when(jnp.logical_not(local))
                def _():
                    remote(src, dst, out_send, out_recv, ff, xx)

        return carry

    lax.fori_loop(0, 16, send_out, 0)

    arounds = [lax.rem(g - 2 * core - k + X, X) for k in range(2)]
    for which, gram in ((1, gright_in), (0, gleft_in)):
        for k in range(2):
            for way in (1, 3):

                @pl.when(arounds[k] == way)
                def _():
                    drain(gram.at[k], gram_recv.at[which, k])
                    drain(relay.at[which], relay_recv.at[which])
                    gg = lax.rem(g + way, X)
                    here = gram.at[k, :, span(g + way)]
                    send = relay_send.at[which]
                    recv = gram_recv.at[which, k]
                    remote(here, cross.at[which, way // 2], send, recv, f, gg)
                    column = span(g + 3)
                    remote(relay.at[which], gram.at[k, :, column], send, recv, f, gg)

    def update(target, gram, k):
        @pl.loop(0, 8)
        def _(m):
            at = pl.ds(pl.multiple_of(m * 32, 32), 32)
            target[k, at] = 0.9 * target[k, at] + 0.1 * gram[k, at].astype(jnp.float32)

    parts = ((1, new_right, gright_in), (0, new_left, gleft_in))
    load_left.wait()
    load_right.wait()
    for last in (False, True):
        for which, target, gram in parts:
            for k in range(2):

                @pl.when((arounds[k] == 2) == last)
                def _():
                    if last:
                        drain(gram.at[k], gram_recv.at[which, k])
                        gram[k, :, span(g + 3)] = cross[which, 0].T
                        gram[k, :, span(g + 1)] = cross[which, 1].T
                    else:

                        @pl.when(arounds[k] == 0)
                        def _():
                            drain(gram.at[k], gram_recv.at[which, k])

                    update(target, gram, k)

    drain(pieces.at[pl.ds(0, QUADS * X - 1)], block_send)
    drain(pieces, swap_send)
    drain(lroot.at[pl.ds(0, 6 * COLS // X)], pass_send)
    drain(norm.at[0], norm_send)
    drain(adam_in.at[0], adam_send.at[0])
    drain(adam_in.at[pl.ds(0, 3)], adam_send.at[1])
    drain(adam_in.at[pl.ds(0, 3)], adam_send.at[2])
    drain(adam_in.at[pl.ds(0, 7)], adam_send.at[3])
    for k in range(2):
        around = lax.rem(g - 2 * core - k + X, X)
        for steps, blocks in ((0, 8), (1, 5), (2, 2), (3, 5)):

            @pl.when(around == steps)
            def _():
                drain(lroot.at[pl.ds(0, blocks * COLS // X)], root_send.at[k])

        around = lax.rem(2 * core + k - g + X, X)
        for which in range(2):

            @pl.when(lax.rem(around, 2) == 1)
            def _():
                drain(gleft.at[k], gram_send.at[which, k])

            @pl.when(around == 2)
            def _():
                drain(relay, gram_send.at[which, k])

    for which in range(2):
        drain(relay, relay_send.at[which])

    @pl.when(at_home)
    def _():
        drain(pieces.at[pl.ds(0, QUADS * X - 1)], out_send)

    @pl.when(jnp.logical_not(at_home))
    def _():
        drain(pieces, out_send)

    drain(returned, out_recv)

    def one_direction(b, carry):
        directions[b] = returned[slot_ref[b]]
        return carry

    lax.fori_loop(0, NBLK, one_direction, 0, unroll=8)


def run_exchange(grads, second_moment, slot_of, block_rows, block_cols, *matrices):
    half = jnp.bfloat16
    away = pl.BlockSpec(memory_space=pl.ANY)
    here = pl.BlockSpec(memory_space=pltpu.VMEM)
    numbers = pl.BlockSpec(memory_space=pltpu.SMEM)
    dma = pltpu.SemaphoreType.DMA
    operands = (slot_of, block_rows, block_cols, grads, second_moment, *matrices)
    return pl.pallas_call(
        exchange,
        out_shape=(
            pltpu.VMEM((NBLK, ROWS, COLS), half),
            pltpu.VMEM((NBLK, ROWS, COLS), jnp.float32),
            pltpu.VMEM((2, COLS, EDGE), jnp.float32),
            pltpu.VMEM((2, COLS, EDGE), jnp.float32),
        ),
        in_specs=[numbers] * 3 + [away] * 6,
        out_specs=(here,) * 4,
        scratch_shapes=[
            pltpu.VMEM((QUADS * X, ROWS, COLS), half),
            pltpu.VMEM((NBLK + 1, ROWS, COLS), half),
            pltpu.VMEM((NBLK, ROWS, COLS), jnp.float32),
            pltpu.VMEM((8, 128), jnp.int32),
            pltpu.SMEM((8, 128), jnp.int32),
            pltpu.VMEM((NBLK, 128), jnp.int32),
            pltpu.VMEM((NBLK, 8, 128), jnp.float32),
            pltpu.VMEM((QUADS * X, ROWS, COLS), half),
            pltpu.VMEM((2, COLS, EDGE), half),
            pltpu.VMEM((2, COLS, EDGE), half),
            pltpu.VMEM((Z, Y, 2, ROWS, EDGE), half),
            pltpu.VMEM((EDGE, EDGE), half),
            pltpu.VMEM((EDGE, EDGE), half),
            pltpu.VMEM((Z, Y, 2, ROWS, HALF), half),
            pltpu.VMEM((EDGE, HALF), jnp.float32),
            pltpu.VMEM((QUADS * 2, ROWS, HALF), half),
            pltpu.VMEM((2, COLS, EDGE), half),
            pltpu.VMEM((2, COLS, EDGE), half),
            pltpu.VMEM((2, COLS, EDGE), jnp.float32),
            pltpu.VMEM((2, COLS, COLS), half),
            pltpu.VMEM((2, 2, COLS, COLS), half),
            pltpu.VMEM((14, 8, 128), jnp.float32),
            pltpu.VMEM((4, 8, 128), jnp.float32),
            pltpu.VMEM((2, 8, 128), jnp.float32),
            dma,
            dma((Y,)),
            dma,
            dma((Y,)),
            dma((2,)),
            dma,
            dma,
            dma,
            dma,
            dma((2, 2)),
            dma((2, 2)),
            dma((2,)),
            dma((2,)),
            dma((4,)),
            dma((4,)),
            dma,
            dma,
            dma,
            dma,
            dma((4,)),
            dma,
            pltpu.SemaphoreType.REGULAR,
        ],
        compiler_params=pltpu.CompilerParams(
            collective_id=0, has_side_effects=True, vmem_limit_bytes=48 * 1024 * 1024
        ),
        cost_estimate=pl.CostEstimate(
            flops=8 * EDGE * EDGE * HALF, bytes_accessed=8 * EDGE * EDGE, transcendentals=0
        ),
    )(*[pltpu.with_memory_space_constraint(operand, pltpu.HBM) for operand in operands])


def solution(mesh):
    placed = (
        P(None, "fsdp", "group"),
        P(None, "fsdp", "group"),
        P(),
        P(),
        P(),
        P("fsdp", "group", None),
        P("fsdp", "group", None),
        P("fsdp", "group", None),
        P("fsdp", None, "group"),
    )
    return jax.shard_map(
        run_exchange,
        mesh=mesh,
        in_specs=placed,
        out_specs=(
            P(None, "fsdp", "group"),
            P(None, "fsdp", "group"),
            P("fsdp", "group", None),
            P("fsdp", "group", None),
        ),
        check_vma=False,
    )
```

```python
import jax
import jax.numpy as jnp
from jax import lax
from jax.experimental import pallas as pl
from jax.experimental.pallas import tpu as pltpu
from jax.sharding import PartitionSpec as P

MESH = pl.DeviceIdType.MESH
Z, Y, X = 8, 4, 4
QUADS = Z * Y
EDGE = 1024
NBLK = 56
HALF = EDGE // 2
ROWS, COLS = 16, 256
FAR_FIRST = (4, 3, 5, 2, 6, 1, 7, 0)


def drain(ref, sem):
    pltpu.make_async_copy(ref, ref, sem).wait()


def exchange(
    slot_ref,
    rows_ref,
    cols_ref,
    grads_ref,
    second_ref,
    lstat_ref,
    rstat_ref,
    lroot_ref,
    rroot_ref,
    directions,
    moments,
    new_left,
    new_right,
    returned,
    grads,
    second,
    table,
    table_smem,
    matches,
    adam_parts,
    pieces,
    gleft_in,
    gright_in,
    block,
    lroot,
    rroot,
    mixed,
    precond,
    direction,
    gleft,
    gright,
    gram_part,
    relay,
    cross,
    adam_in,
    adam_sum,
    norm,
    block_send,
    block_recv,
    swap_send,
    swap_recv,
    root_send,
    root_recv,
    row_recv,
    pass_send,
    pass_recv,
    gram_send,
    gram_recv,
    relay_send,
    relay_recv,
    adam_send,
    adam_recv,
    norm_send,
    norm_recv,
    out_send,
    out_recv,
    load_sem,
    table_sem,
):
    f = lax.axis_index("fsdp")
    g = lax.axis_index("group")
    core = lax.rem(f, 2)
    quad = lax.div(f, 2)
    y = lax.rem(quad, Y)
    z = lax.div(quad, Y)
    slot = quad * X + g
    other = f + 1 - 2 * core
    side = lax.div(g, 2)
    parity = lax.rem(g, 2)
    at_home = side == core

    def device(zz, yy, cc):
        return (zz * Y + yy) * 2 + cc

    def remote(src, dst, send, recv, ff, gg):
        pltpu.make_async_remote_copy(
            src_ref=src,
            dst_ref=dst,
            send_sem=send,
            recv_sem=recv,
            device_id=(ff, gg),
            device_id_type=MESH,
        ).start()

    def span(j):
        return pl.ds(pl.multiple_of(lax.rem(j, X) * COLS, COLS), COLS)

    def left_block(ref, j, k):
        return ref.at[span(j), span(k)]

    def send_root(k, ff, xx, lefts, rights):
        for d in lefts:
            src = lroot_ref.at[k, :, span(g + d)]
            remote(src, left_block(lroot, g, g + d), root_send.at[k], root_recv, ff, xx)
        for d in rights:
            src = rroot_ref.at[k, span(g + d), :]
            remote(src, left_block(rroot, g + d, g), root_send.at[k], root_recv, ff, xx)

    def send_roots():
        for k in range(2):
            home = 2 * core + k
            around = lax.rem(g - home + X, X)

            @pl.when(around == 0)
            def _():
                for src, dst in ((lroot_ref.at[k], lroot.at[span(g)]), (rroot_ref.at[k], rroot.at[:, span(g)])):
                    remote(src, dst, root_send.at[k], row_recv, other, g)
                    pltpu.make_async_copy(src, dst, row_recv).start()

            @pl.when(around == 1)
            def _():
                send_root(k, quad * 2, home, (0, 1, 2), (0, 1))

            @pl.when(around == 2)
            def _():
                send_root(k, quad * 2, home, (0,), ())
                send_root(k, quad * 2 + 1, home, (), (0,))

            @pl.when(around == 3)
            def _():
                send_root(k, quad * 2 + 1, home, (0, 3), (0, 3, 2))

    load_grads = pltpu.make_async_copy(grads_ref, grads.at[pl.ds(0, NBLK)], load_sem.at[0])
    load_second = pltpu.make_async_copy(second_ref, second, load_sem.at[1])
    load_left = pltpu.make_async_copy(lstat_ref, new_left, load_sem.at[2])
    load_right = pltpu.make_async_copy(rstat_ref, new_right, load_sem.at[3])
    load_grads.start()
    load_second.start()
    barrier = pltpu.get_barrier_semaphore()

    def greet(ff, gg):
        pl.semaphore_signal(barrier, inc=1, device_id=(ff, gg), device_id_type=MESH)

    for d in range(X):
        greet(other, lax.rem(g + d, X))
        if d:
            greet(f, lax.rem(g + d, X))

    @pl.loop(1, QUADS)
    def _(n):
        for d in range(X):
            greet(lax.rem(quad + n, QUADS) * 2 + core, lax.rem(g + d, X))

    lane = lax.broadcasted_iota(jnp.int32, (8, 128), 1)

    def valid(b):
        return (f * ROWS < rows_ref[b]) & (g * COLS < cols_ref[b])

    source = jnp.full((8, 128), NBLK, jnp.int32)
    for b in range(NBLK):
        match = lane == slot_ref[b]
        source = jnp.where(match, jnp.where(valid(b), b, NBLK), source)
        matches[pl.ds(b, 1)] = match[0:1].astype(jnp.int32)
    table[...] = source
    to_smem = pltpu.make_async_copy(table, table_smem, table_sem)
    to_smem.start()
    grads[NBLK] = jnp.zeros((ROWS, COLS), jnp.bfloat16)
    to_smem.wait()
    load_grads.wait()

    mine = block.at[z, y, core, :, pl.ds(pl.multiple_of(g * COLS, COLS), COLS)]

    @pl.loop(0, QUADS * X // 8)
    def _(n):
        for k in range(8):
            pieces[n * 8 + k] = grads[table_smem[0, n * 8 + k]]

    pl.semaphore_wait(barrier, QUADS * X + 3)
    send_roots()

    def send_blocks(step, carry):
        dy, dx = lax.div(step, X), lax.rem(step, X)
        yy, xx = lax.rem(y + dy, Y), lax.rem(g + dx, X)
        for dz in FAR_FIRST:
            zz = lax.rem(z + dz, Z)
            at = (zz * Y + yy) * X + xx
            src = pieces.at[at]
            if dz:
                remote(src, mine, block_send, block_recv.at[dy], device(zz, yy, core), xx)
            else:

                @pl.when(step == 0)
                def _():
                    pltpu.make_async_copy(src, mine, block_recv.at[0]).start()

                @pl.when(step != 0)
                def _():
                    remote(src, mine, block_send, block_recv.at[dy], device(zz, yy, core), xx)

        return carry

    lax.fori_loop(0, X * Y, send_blocks, 0)

    load_left.start()
    load_right.start()

    load_second.wait()

    def one_block(b, carry):
        grad = jnp.where(valid(b), grads[b].astype(jnp.float32), 0.0)
        moment = 0.95 * second[b] + 0.05 * grad * grad
        moments[b] = moment
        adam = grad / (jnp.sqrt(moment) + 1e-08)
        adam = adam * adam
        adam = adam[0:8] + adam[8:16]
        adam_parts[b] = adam[:, 0:128] + adam[:, 128:256]
        return carry

    lax.fori_loop(0, NBLK, one_block, 0, unroll=4)
    adam = jnp.sum(jnp.sum(adam_parts[...], axis=1), axis=1, keepdims=True)
    adam = jnp.where(matches[...] != 0, adam, 0.0)
    adam_sum[0] = jnp.broadcast_to(jnp.sum(adam, axis=0, keepdims=True), (8, 128))

    def adam_stage(stage, first, peers):
        for d, (ff, gg) in enumerate(peers):
            remote(adam_sum.at[stage], adam_in.at[first + d], adam_send.at[stage], adam_recv.at[stage], ff, gg)

    def adam_add(stage, first, count):
        drain(adam_in.at[pl.ds(first, count)], adam_recv.at[stage])
        total = adam_sum[stage]
        for d in range(count):
            total = total + adam_in[first + d]
        return total

    adam_stage(0, 0, [(other, g)])

    def pass_on(ref, j, k):
        here = left_block(ref, j, k)
        remote(here, here, pass_send, pass_recv, other, g)

    half = pl.ds(pl.multiple_of(core * HALF, HALF), HALF)

    def send_gram(which, m, src, dst):
        xx = 2 * core + m
        ff = quad * 2 + side
        around = lax.rem(xx - g + X, X)
        send = gram_send.at[which, m]

        @pl.when(around == 0)
        def _():
            pltpu.make_async_copy(src.at[m], dst.at[parity], gram_recv.at[which, parity]).start()

        @pl.when(lax.rem(around, 2) == 1)
        def _():
            remote(src.at[m], dst.at[parity], send, gram_recv.at[which, parity], ff, xx)

        @pl.when(around == 2)
        def _():
            for d, gg in ((0, lax.rem(g + 1, X)), (2, lax.rem(g + 3, X))):
                remote(src.at[m, :, span(g + d)], relay.at[which], send, relay_recv.at[which], ff, gg)

    def swap(d):
        ys = lax.rem(y + Y - d, Y)
        rows = block.at[:, ys, core]
        drain(rows, block_recv.at[d])
        remote(rows, rows, swap_send, swap_recv.at[d], other, g)

    def gram(d):
        ys = lax.rem(y + Y - d, Y)
        drain(block.at[:, ys, 1 - core], swap_recv.at[d])
        for m in range(2):
            at = pl.multiple_of(core * HALF + m * COLS, COLS)
            value = lax.dot_general(
                block[:, ys, :, :, pl.ds(at, COLS)].reshape(COLS, COLS),
                block[:, ys].reshape(COLS, EDGE),
                (((0,), (0,)), ((), ())),
                preferred_element_type=jnp.float32,
            )
            if d:
                value = gram_part[m] + value
            if d < Y - 1:
                gram_part[m] = value
            else:
                gright[m] = value.astype(jnp.bfloat16)
                send_gram(1, m, gright, gright_in)

    def mix(d):
        ys = lax.rem(y + Y - d, Y)
        value = jnp.dot(
            block[:, ys].reshape(COLS, EDGE), rroot[:, half], preferred_element_type=jnp.float32
        )
        mixed[:, ys] = value.astype(jnp.bfloat16).reshape(Z, 2, ROWS, HALF)

    swap(0)
    swap(1)
    gram(0)

    drain(lroot.at[pl.ds(0, 6 * COLS // X)], root_recv)

    @pl.when(core == 0)
    def _():
        for ref, j, k in ((lroot, 1, 1), (lroot, 1, 2), (lroot, 1, 3), (lroot, 2, 2), (rroot, 1, 1), (rroot, 2, 1)):
            pass_on(ref, g + j, g + k)

    @pl.when(core == 1)
    def _():
        for ref, j, k in ((lroot, 3, 3), (lroot, 3, 2), (rroot, 3, 3), (rroot, 2, 3), (rroot, 1, 3), (rroot, 2, 2)):
            pass_on(ref, g + j, g + k)

    adam_sum[1] = adam_add(0, 0, 1)
    adam_stage(1, 1, [(f, lax.rem(g + d, X)) for d in range(1, X)])
    gram(1)

    drain(lroot.at[pl.ds(0, 2 * COLS)], row_recv)
    drain(lroot.at[pl.ds(0, 6 * COLS // X)], pass_recv)
    for j, k in ((1, 0), (2, 0), (3, 0), (2, 1), (2, 3), (1, 3)):
        rroot[span(g + k), span(g + j)] = rroot[span(g + j), span(g + k)].T
    for j, k in ((0, 1), (0, 2), (0, 3), (1, 2), (3, 2), (1, 3)):
        lroot[span(g + k), span(g + j)] = lroot[span(g + j), span(g + k)].T

    swap(2)
    gram(2)
    adam_sum[2] = adam_add(1, 1, X - 1)
    adam_stage(2, 4, [(device(z, lax.rem(y + d, Y), core), g) for d in range(1, Y)])
    swap(3)
    for d in range(3):
        mix(d)
    gram(3)
    mix(3)
    adam_sum[3] = adam_add(2, 4, Y - 1)
    adam_stage(3, 7, [(device(lax.rem(z + d, Z), y, core), g) for d in range(1, Z)])

    rows_valid, cols_valid = 0, 0
    for b in range(NBLK):
        rows_valid = jnp.where(slot_ref[b] == slot, rows_ref[b], rows_valid)
        cols_valid = jnp.where(slot_ref[b] == slot, cols_ref[b], cols_valid)
    cols_keep = (core * HALF + lax.broadcasted_iota(jnp.int32, (COLS, HALF), 1)) < cols_valid

    def one_part(m, total):
        at = pl.multiple_of(m * COLS, COLS)
        value = jnp.dot(lroot[pl.ds(at, COLS)], mixed[...].reshape(EDGE, HALF), preferred_element_type=jnp.float32)
        rows_keep = (at + lax.broadcasted_iota(jnp.int32, (COLS, HALF), 0)) < rows_valid
        value = jnp.where(rows_keep & cols_keep, value, 0.0)
        precond[pl.ds(at, COLS)] = value
        square = value * value
        return total + jnp.sum(square.reshape(COLS // 8, 8, HALF), axis=0)

    total = lax.fori_loop(0, 4, one_part, jnp.zeros((8, HALF), jnp.float32))
    norm[0] = jnp.broadcast_to(jnp.sum(total, keepdims=True), (8, 128))
    remote(norm.at[0], norm.at[1], norm_send, norm_recv, other, g)

    for m in range(2):
        gleft[m] = lax.dot_general(
            block[pl.ds(core * 4 + m * 2, 2)].reshape(COLS, EDGE),
            block[...].reshape(EDGE, EDGE),
            (((1,), (1,)), ((), ())),
            preferred_element_type=jnp.float32,
        ).astype(jnp.bfloat16)
        send_gram(0, m, gleft, gleft_in)

    adam = adam_add(3, 7, Z - 1)
    adam = jnp.sum(jnp.where(lane == slot, adam, 0.0)[0:1], keepdims=True)

    drain(norm.at[1], norm_recv)
    squares = (norm[0] + norm[1])[0:1, 0:1]
    factor = jnp.sqrt(adam) / (jnp.sqrt(squares) + 1e-06)

    @pl.loop(0, 4)
    def _(m):
        at = pl.multiple_of(m * COLS, COLS)
        value = (precond[pl.ds(at, COLS)] * factor).astype(jnp.bfloat16)
        direction[pl.ds(m * 16, 16)] = value.reshape(16, ROWS, HALF)

    def send_out(step, carry):
        dy, dc, e = lax.div(step, 4), lax.rem(lax.div(step, 2), 2), lax.rem(step, 2)
        yy, cc, xx = lax.rem(y + dy, Y), lax.rem(core + dc, 2), 2 * core + e
        for dz in FAR_FIRST:
            ff = device(lax.rem(z + dz, Z), yy, cc)
            src = direction.at[ff, :, pl.ds(pl.multiple_of(e * COLS, COLS), COLS)]
            dst = returned.at[slot]
            if dz:
                remote(src, dst, out_send, out_recv, ff, xx)
            else:
                local = (step < 2) & at_home & (parity == e)

                @pl.when(local)
                def _():
                    pltpu.make_async_copy(src, dst, out_recv).start()

                @pl.when(jnp.logical_not(local))
                def _():
                    remote(src, dst, out_send, out_recv, ff, xx)

        return carry

    lax.fori_loop(0, 16, send_out, 0)

    arounds = [lax.rem(g - 2 * core - k + X, X) for k in range(2)]
    for which, gram in ((1, gright_in), (0, gleft_in)):
        for k in range(2):
            for way in (1, 3):

                @pl.when(arounds[k] == way)
                def _():
                    drain(gram.at[k], gram_recv.at[which, k])
                    drain(relay.at[which], relay_recv.at[which])
                    gg = lax.rem(g + way, X)
                    here = gram.at[k, :, span(g + way)]
                    send = relay_send.at[which]
                    recv = gram_recv.at[which, k]
                    remote(here, cross.at[which, way // 2], send, recv, f, gg)
                    column = span(g + 3)
                    remote(relay.at[which], gram.at[k, :, column], send, recv, f, gg)

    def update(target, gram, k):
        @pl.loop(0, 8)
        def _(m):
            at = pl.ds(pl.multiple_of(m * 32, 32), 32)
            target[k, at] = 0.9 * target[k, at] + 0.1 * gram[k, at].astype(jnp.float32)

    parts = ((1, new_right, gright_in), (0, new_left, gleft_in))
    load_left.wait()
    load_right.wait()
    for last in (False, True):
        for which, target, gram in parts:
            for k in range(2):

                @pl.when((arounds[k] == 2) == last)
                def _():
                    if last:
                        drain(gram.at[k], gram_recv.at[which, k])
                        gram[k, :, span(g + 3)] = cross[which, 0].T
                        gram[k, :, span(g + 1)] = cross[which, 1].T
                    else:

                        @pl.when(arounds[k] == 0)
                        def _():
                            drain(gram.at[k], gram_recv.at[which, k])

                    update(target, gram, k)

    drain(pieces.at[pl.ds(0, QUADS * X - 1)], block_send)
    drain(pieces, swap_send)
    drain(lroot.at[pl.ds(0, 6 * COLS // X)], pass_send)
    drain(norm.at[0], norm_send)
    drain(adam_in.at[0], adam_send.at[0])
    drain(adam_in.at[pl.ds(0, 3)], adam_send.at[1])
    drain(adam_in.at[pl.ds(0, 3)], adam_send.at[2])
    drain(adam_in.at[pl.ds(0, 7)], adam_send.at[3])
    for k in range(2):
        around = lax.rem(g - 2 * core - k + X, X)
        for steps, blocks in ((0, 8), (1, 5), (2, 2), (3, 5)):

            @pl.when(around == steps)
            def _():
                drain(lroot.at[pl.ds(0, blocks * COLS // X)], root_send.at[k])

        around = lax.rem(2 * core + k - g + X, X)
        for which in range(2):

            @pl.when(lax.rem(around, 2) == 1)
            def _():
                drain(gleft.at[k], gram_send.at[which, k])

            @pl.when(around == 2)
            def _():
                drain(relay, gram_send.at[which, k])

    for which in range(2):
        drain(relay, relay_send.at[which])

    @pl.when(at_home)
    def _():
        drain(pieces.at[pl.ds(0, QUADS * X - 1)], out_send)

    @pl.when(jnp.logical_not(at_home))
    def _():
        drain(pieces, out_send)

    drain(returned, out_recv)

    def one_direction(b, carry):
        directions[b] = returned[slot_ref[b]]
        return carry

    lax.fori_loop(0, NBLK, one_direction, 0, unroll=8)


def run_exchange(grads, second_moment, slot_of, block_rows, block_cols, *matrices):
    half = jnp.bfloat16
    away = pl.BlockSpec(memory_space=pl.ANY)
    here = pl.BlockSpec(memory_space=pltpu.VMEM)
    numbers = pl.BlockSpec(memory_space=pltpu.SMEM)
    dma = pltpu.SemaphoreType.DMA
    operands = (slot_of, block_rows, block_cols, grads, second_moment, *matrices)
    return pl.pallas_call(
        exchange,
        out_shape=(
            pltpu.VMEM((NBLK, ROWS, COLS), half),
            pltpu.VMEM((NBLK, ROWS, COLS), jnp.float32),
            pltpu.VMEM((2, COLS, EDGE), jnp.float32),
            pltpu.VMEM((2, COLS, EDGE), jnp.float32),
        ),
        in_specs=[numbers] * 3 + [away] * 6,
        out_specs=(here,) * 4,
        scratch_shapes=[
            pltpu.VMEM((QUADS * X, ROWS, COLS), half),
            pltpu.VMEM((NBLK + 1, ROWS, COLS), half),
            pltpu.VMEM((NBLK, ROWS, COLS), jnp.float32),
            pltpu.VMEM((8, 128), jnp.int32),
            pltpu.SMEM((8, 128), jnp.int32),
            pltpu.VMEM((NBLK, 128), jnp.int32),
            pltpu.VMEM((NBLK, 8, 128), jnp.float32),
            pltpu.VMEM((QUADS * X, ROWS, COLS), half),
            pltpu.VMEM((2, COLS, EDGE), half),
            pltpu.VMEM((2, COLS, EDGE), half),
            pltpu.VMEM((Z, Y, 2, ROWS, EDGE), half),
            pltpu.VMEM((EDGE, EDGE), half),
            pltpu.VMEM((EDGE, EDGE), half),
            pltpu.VMEM((Z, Y, 2, ROWS, HALF), half),
            pltpu.VMEM((EDGE, HALF), jnp.float32),
            pltpu.VMEM((QUADS * 2, ROWS, HALF), half),
            pltpu.VMEM((2, COLS, EDGE), half),
            pltpu.VMEM((2, COLS, EDGE), half),
            pltpu.VMEM((2, COLS, EDGE), jnp.float32),
            pltpu.VMEM((2, COLS, COLS), half),
            pltpu.VMEM((2, 2, COLS, COLS), half),
            pltpu.VMEM((14, 8, 128), jnp.float32),
            pltpu.VMEM((4, 8, 128), jnp.float32),
            pltpu.VMEM((2, 8, 128), jnp.float32),
            dma,
            dma((Y,)),
            dma,
            dma((Y,)),
            dma((2,)),
            dma,
            dma,
            dma,
            dma,
            dma((2, 2)),
            dma((2, 2)),
            dma((2,)),
            dma((2,)),
            dma((4,)),
            dma((4,)),
            dma,
            dma,
            dma,
            dma,
            dma((4,)),
            dma,
        ],
        compiler_params=pltpu.CompilerParams(
            collective_id=0, has_side_effects=True, vmem_limit_bytes=48 * 1024 * 1024
        ),
        cost_estimate=pl.CostEstimate(
            flops=8 * EDGE * EDGE * HALF, bytes_accessed=8 * EDGE * EDGE, transcendentals=0
        ),
    )(*[pltpu.with_memory_space_constraint(operand, pltpu.HBM) for operand in operands])


def solution(mesh):
    placed = (
        P(None, "fsdp", "group"),
        P(None, "fsdp", "group"),
        P(),
        P(),
        P(),
        P("fsdp", "group", None),
        P("fsdp", "group", None),
        P("fsdp", "group", None),
        P("fsdp", None, "group"),
    )
    return jax.shard_map(
        run_exchange,
        mesh=mesh,
        in_specs=placed,
        out_specs=(
            P(None, "fsdp", "group"),
            P(None, "fsdp", "group"),
            P("fsdp", "group", None),
            P("fsdp", "group", None),
        ),
        check_vma=False,
    )
```

```python
import jax
import jax.numpy as jnp
from jax import lax
from jax.experimental import pallas as pl
from jax.experimental.pallas import tpu as pltpu
from jax.sharding import PartitionSpec as P

MESH = pl.DeviceIdType.MESH
Z, Y, X = 8, 4, 4
QUADS = Z * Y
EDGE = 1024
NBLK = 56
HALF = EDGE // 2
ROWS, COLS = 16, 256
FAR_FIRST = (4, 3, 5, 2, 6, 1, 7, 0)


def drain(ref, sem):
    pltpu.make_async_copy(ref, ref, sem).wait()


def exchange(
    slot_ref,
    rows_ref,
    cols_ref,
    grads_ref,
    second_ref,
    lstat_ref,
    rstat_ref,
    lroot_ref,
    rroot_ref,
    directions,
    moments,
    new_left,
    new_right,
    returned,
    grads,
    second,
    table,
    table_smem,
    matches,
    adam_parts,
    pieces,
    gleft_in,
    gright_in,
    block,
    lroot,
    rroot,
    mixed,
    precond,
    direction,
    gleft,
    gright,
    gram_part,
    relay,
    cross,
    adam_in,
    adam_sum,
    norm,
    block_send,
    block_recv,
    swap_send,
    swap_recv,
    root_send,
    root_recv,
    row_recv,
    pass_send,
    pass_recv,
    gram_send,
    gram_recv,
    relay_send,
    relay_recv,
    adam_send,
    adam_recv,
    norm_send,
    norm_recv,
    out_send,
    out_recv,
    load_sem,
    table_sem,
):
    f = lax.axis_index("fsdp")
    g = lax.axis_index("group")
    core = lax.rem(f, 2)
    quad = lax.div(f, 2)
    y = lax.rem(quad, Y)
    z = lax.div(quad, Y)
    slot = quad * X + g
    other = f + 1 - 2 * core
    side = lax.div(g, 2)
    parity = lax.rem(g, 2)
    at_home = side == core

    def device(zz, yy, cc):
        return (zz * Y + yy) * 2 + cc

    def remote(src, dst, send, recv, ff, gg):
        pltpu.make_async_remote_copy(
            src_ref=src,
            dst_ref=dst,
            send_sem=send,
            recv_sem=recv,
            device_id=(ff, gg),
            device_id_type=MESH,
        ).start()

    def span(j):
        return pl.ds(pl.multiple_of(lax.rem(j, X) * COLS, COLS), COLS)

    def left_block(ref, j, k):
        return ref.at[span(j), span(k)]

    def send_root(k, ff, xx, lefts, rights):
        for d in lefts:
            src = lroot_ref.at[k, :, span(g + d)]
            remote(src, left_block(lroot, g, g + d), root_send.at[k], root_recv, ff, xx)
        for d in rights:
            src = rroot_ref.at[k, span(g + d), :]
            remote(src, left_block(rroot, g + d, g), root_send.at[k], root_recv, ff, xx)

    def send_roots():
        for k in range(2):
            home = 2 * core + k
            around = lax.rem(g - home + X, X)

            @pl.when(around == 0)
            def _():
                for src, dst in ((lroot_ref.at[k], lroot.at[span(g)]), (rroot_ref.at[k], rroot.at[:, span(g)])):
                    remote(src, dst, root_send.at[k], row_recv, other, g)
                    pltpu.make_async_copy(src, dst, row_recv).start()

            @pl.when(around == 1)
            def _():
                send_root(k, quad * 2, home, (0, 1, 2), (0, 1))

            @pl.when(around == 2)
            def _():
                send_root(k, quad * 2, home, (0,), ())
                send_root(k, quad * 2 + 1, home, (), (0,))

            @pl.when(around == 3)
            def _():
                send_root(k, quad * 2 + 1, home, (0, 3), (0, 3, 2))

    load_grads = pltpu.make_async_copy(grads_ref, grads.at[pl.ds(0, NBLK)], load_sem.at[0])
    load_second = pltpu.make_async_copy(second_ref, second, load_sem.at[1])
    load_left = pltpu.make_async_copy(lstat_ref, new_left, load_sem.at[2])
    load_right = pltpu.make_async_copy(rstat_ref, new_right, load_sem.at[3])
    load_grads.start()
    load_second.start()
    barrier = pltpu.get_barrier_semaphore()

    def greet(ff, gg):
        pl.semaphore_signal(barrier, inc=1, device_id=(ff, gg), device_id_type=MESH)

    for d in range(X):
        greet(other, lax.rem(g + d, X))
        if d:
            greet(f, lax.rem(g + d, X))

    @pl.loop(1, QUADS)
    def _(n):
        for d in range(X):
            greet(lax.rem(quad + n, QUADS) * 2 + core, lax.rem(g + d, X))

    lane = lax.broadcasted_iota(jnp.int32, (8, 128), 1)

    def valid(b):
        return (f * ROWS < rows_ref[b]) & (g * COLS < cols_ref[b])

    source = jnp.full((8, 128), NBLK, jnp.int32)
    for b in range(NBLK):
        match = lane == slot_ref[b]
        source = jnp.where(match, jnp.where(valid(b), b, NBLK), source)
        matches[pl.ds(b, 1)] = match[0:1].astype(jnp.int32)
    table[...] = source
    to_smem = pltpu.make_async_copy(table, table_smem, table_sem)
    to_smem.start()
    grads[NBLK] = jnp.zeros((ROWS, COLS), jnp.bfloat16)
    to_smem.wait()
    load_grads.wait()

    mine = block.at[z, y, core, :, pl.ds(pl.multiple_of(g * COLS, COLS), COLS)]

    @pl.loop(0, QUADS * X // 8)
    def _(n):
        for k in range(8):
            pieces[n * 8 + k] = grads[table_smem[0, n * 8 + k]]

    pl.semaphore_wait(barrier, QUADS * X + 3)
    send_roots()

    def send_blocks(step, carry):
        dy, dx = lax.div(step, X), lax.rem(step, X)
        yy, xx = lax.rem(y + dy, Y), lax.rem(g + dx, X)
        for dz in FAR_FIRST:
            zz = lax.rem(z + dz, Z)
            at = (zz * Y + yy) * X + xx
            src = pieces.at[at]
            if dz:
                remote(src, mine, block_send, block_recv.at[dy], device(zz, yy, core), xx)
            else:

                @pl.when(step == 0)
                def _():
                    pltpu.make_async_copy(src, mine, block_recv.at[0]).start()

                @pl.when(step != 0)
                def _():
                    remote(src, mine, block_send, block_recv.at[dy], device(zz, yy, core), xx)

        return carry

    lax.fori_loop(0, X * Y, send_blocks, 0)

    load_left.start()
    load_right.start()

    load_second.wait()

    def one_block(b, carry):
        grad = jnp.where(valid(b), grads[b].astype(jnp.float32), 0.0)
        moment = 0.95 * second[b] + 0.05 * grad * grad
        moments[b] = moment
        adam = grad / (jnp.sqrt(moment) + 1e-08)
        adam = adam * adam
        adam = adam[0:8] + adam[8:16]
        adam_parts[b] = adam[:, 0:128] + adam[:, 128:256]
        return carry

    lax.fori_loop(0, NBLK, one_block, 0, unroll=4)
    adam = jnp.sum(jnp.sum(adam_parts[...], axis=1), axis=1, keepdims=True)
    adam = jnp.where(matches[...] != 0, adam, 0.0)
    adam_sum[0] = jnp.broadcast_to(jnp.sum(adam, axis=0, keepdims=True), (8, 128))

    def adam_stage(stage, first, peers):
        for d, (ff, gg) in enumerate(peers):
            remote(adam_sum.at[stage], adam_in.at[first + d], adam_send.at[stage], adam_recv.at[stage], ff, gg)

    def adam_add(stage, first, count):
        drain(adam_in.at[pl.ds(first, count)], adam_recv.at[stage])
        total = adam_sum[stage]
        for d in range(count):
            total = total + adam_in[first + d]
        return total

    adam_stage(0, 0, [(other, g)])

    def pass_on(ref, j, k):
        here = left_block(ref, j, k)
        remote(here, here, pass_send, pass_recv, other, g)

    half = pl.ds(pl.multiple_of(core * HALF, HALF), HALF)

    def send_gram(which, m, src, dst):
        xx = 2 * core + m
        ff = quad * 2 + side
        around = lax.rem(xx - g + X, X)
        send = gram_send.at[which, m]

        @pl.when(around == 0)
        def _():
            pltpu.make_async_copy(src.at[m], dst.at[parity], gram_recv.at[which, parity]).start()

        @pl.when(lax.rem(around, 2) == 1)
        def _():
            remote(src.at[m], dst.at[parity], send, gram_recv.at[which, parity], ff, xx)

        @pl.when(around == 2)
        def _():
            for d, gg in ((0, lax.rem(g + 1, X)), (2, lax.rem(g + 3, X))):
                remote(src.at[m, :, span(g + d)], relay.at[which], send, relay_recv.at[which], ff, gg)

    def swap(d):
        ys = lax.rem(y + Y - d, Y)
        rows = block.at[:, ys, core]
        drain(rows, block_recv.at[d])
        remote(rows, rows, swap_send, swap_recv.at[d], other, g)

    def gram(d):
        ys = lax.rem(y + Y - d, Y)
        drain(block.at[:, ys, 1 - core], swap_recv.at[d])
        for m in range(2):
            at = pl.multiple_of(core * HALF + m * COLS, COLS)
            value = lax.dot_general(
                block[:, ys, :, :, pl.ds(at, COLS)].reshape(COLS, COLS),
                block[:, ys].reshape(COLS, EDGE),
                (((0,), (0,)), ((), ())),
                preferred_element_type=jnp.float32,
            )
            if d:
                value = gram_part[m] + value
            if d < Y - 1:
                gram_part[m] = value
            else:
                gright[m] = value.astype(jnp.bfloat16)
                send_gram(1, m, gright, gright_in)

    def mix(d):
        ys = lax.rem(y + Y - d, Y)
        value = jnp.dot(
            block[:, ys].reshape(COLS, EDGE), rroot[:, half], preferred_element_type=jnp.float32
        )
        mixed[:, ys] = value.astype(jnp.bfloat16).reshape(Z, 2, ROWS, HALF)

    swap(0)
    swap(1)
    gram(0)

    drain(lroot.at[pl.ds(0, 6 * COLS // X)], root_recv)

    @pl.when(core == 0)
    def _():
        for ref, j, k in ((lroot, 1, 1), (lroot, 1, 2), (lroot, 1, 3), (lroot, 2, 2), (rroot, 1, 1), (rroot, 2, 1)):
            pass_on(ref, g + j, g + k)

    @pl.when(core == 1)
    def _():
        for ref, j, k in ((lroot, 3, 3), (lroot, 3, 2), (rroot, 3, 3), (rroot, 2, 3), (rroot, 1, 3), (rroot, 2, 2)):
            pass_on(ref, g + j, g + k)

    adam_sum[1] = adam_add(0, 0, 1)
    adam_stage(1, 1, [(f, lax.rem(g + d, X)) for d in range(1, X)])
    gram(1)

    drain(lroot.at[pl.ds(0, 2 * COLS)], row_recv)
    drain(lroot.at[pl.ds(0, 6 * COLS // X)], pass_recv)
    for j, k in ((1, 0), (2, 0), (3, 0), (2, 1), (2, 3), (1, 3)):
        rroot[span(g + k), span(g + j)] = rroot[span(g + j), span(g + k)].T
    for j, k in ((0, 1), (0, 2), (0, 3), (1, 2), (3, 2), (1, 3)):
        lroot[span(g + k), span(g + j)] = lroot[span(g + j), span(g + k)].T

    swap(2)
    gram(2)
    adam_sum[2] = adam_add(1, 1, X - 1)
    adam_stage(2, 4, [(device(z, lax.rem(y + d, Y), core), g) for d in range(1, Y)])
    swap(3)
    for d in range(3):
        mix(d)
    gram(3)
    mix(3)
    adam_sum[3] = adam_add(2, 4, Y - 1)
    adam_stage(3, 7, [(device(lax.rem(z + d, Z), y, core), g) for d in range(1, Z)])

    rows_valid, cols_valid = 0, 0
    for b in range(NBLK):
        rows_valid = jnp.where(slot_ref[b] == slot, rows_ref[b], rows_valid)
        cols_valid = jnp.where(slot_ref[b] == slot, cols_ref[b], cols_valid)
    cols_keep = (core * HALF + lax.broadcasted_iota(jnp.int32, (COLS, HALF), 1)) < cols_valid

    def one_part(m, total):
        at = pl.multiple_of(m * COLS, COLS)
        value = jnp.dot(lroot[pl.ds(at, COLS)], mixed[...].reshape(EDGE, HALF), preferred_element_type=jnp.float32)
        rows_keep = (at + lax.broadcasted_iota(jnp.int32, (COLS, HALF), 0)) < rows_valid
        value = jnp.where(rows_keep & cols_keep, value, 0.0)
        precond[pl.ds(at, COLS)] = value
        square = value * value
        return total + jnp.sum(square.reshape(COLS // 8, 8, HALF), axis=0)

    total = lax.fori_loop(0, 4, one_part, jnp.zeros((8, HALF), jnp.float32))
    norm[0] = jnp.broadcast_to(jnp.sum(total, keepdims=True), (8, 128))
    remote(norm.at[0], norm.at[1], norm_send, norm_recv, other, g)

    for m in range(2):
        gleft[m] = lax.dot_general(
            block[pl.ds(core * 4 + m * 2, 2)].reshape(COLS, EDGE),
            block[...].reshape(EDGE, EDGE),
            (((1,), (1,)), ((), ())),
            preferred_element_type=jnp.float32,
        ).astype(jnp.bfloat16)
        send_gram(0, m, gleft, gleft_in)

    adam = adam_add(3, 7, Z - 1)
    adam = jnp.sum(jnp.where(lane == slot, adam, 0.0)[0:1], keepdims=True)

    drain(norm.at[1], norm_recv)
    squares = (norm[0] + norm[1])[0:1, 0:1]
    factor = jnp.sqrt(adam) / (jnp.sqrt(squares) + 1e-06)

    @pl.loop(0, 4)
    def _(m):
        at = pl.multiple_of(m * COLS, COLS)
        value = (precond[pl.ds(at, COLS)] * factor).astype(jnp.bfloat16)
        direction[pl.ds(m * 16, 16)] = value.reshape(16, ROWS, HALF)

    def send_out(step, carry):
        dy, dc, e = lax.div(step, 4), lax.rem(lax.div(step, 2), 2), lax.rem(step, 2)
        yy, cc, xx = lax.rem(y + dy, Y), lax.rem(core + dc, 2), 2 * core + e
        for dz in FAR_FIRST:
            ff = device(lax.rem(z + dz, Z), yy, cc)
            src = direction.at[ff, :, pl.ds(pl.multiple_of(e * COLS, COLS), COLS)]
            dst = returned.at[slot]
            if dz:
                remote(src, dst, out_send, out_recv, ff, xx)
            else:
                local = (step < 2) & at_home & (parity == e)

                @pl.when(local)
                def _():
                    pltpu.make_async_copy(src, dst, out_recv).start()

                @pl.when(jnp.logical_not(local))
                def _():
                    remote(src, dst, out_send, out_recv, ff, xx)

        return carry

    lax.fori_loop(0, 16, send_out, 0)

    arounds = [lax.rem(g - 2 * core - k + X, X) for k in range(2)]
    for which, gram in ((1, gright_in), (0, gleft_in)):
        for k in range(2):
            for way in (1, 3):

                @pl.when(arounds[k] == way)
                def _():
                    drain(gram.at[k], gram_recv.at[which, k])
                    drain(relay.at[which], relay_recv.at[which])
                    gg = lax.rem(g + way, X)
                    here = gram.at[k, :, span(g + way)]
                    send = relay_send.at[which]
                    recv = gram_recv.at[which, k]
                    remote(here, cross.at[which, way // 2], send, recv, f, gg)
                    column = span(g + 3)
                    remote(relay.at[which], gram.at[k, :, column], send, recv, f, gg)

    def update(target, gram, k):
        @pl.loop(0, 8)
        def _(m):
            at = pl.ds(pl.multiple_of(m * 32, 32), 32)
            target[k, at] = 0.9 * target[k, at] + 0.1 * gram[k, at].astype(jnp.float32)

    parts = ((1, new_right, gright_in), (0, new_left, gleft_in))
    load_left.wait()
    load_right.wait()
    for last in (False, True):
        for which, target, gram in parts:
            for k in range(2):

                @pl.when((arounds[k] == 2) == last)
                def _():
                    if last:
                        drain(gram.at[k], gram_recv.at[which, k])
                        gram[k, :, span(g + 3)] = cross[which, 0].T
                        gram[k, :, span(g + 1)] = cross[which, 1].T
                    else:

                        @pl.when(arounds[k] == 0)
                        def _():
                            drain(gram.at[k], gram_recv.at[which, k])

                    update(target, gram, k)

    drain(pieces.at[pl.ds(0, QUADS * X - 1)], block_send)
    drain(pieces, swap_send)
    drain(lroot.at[pl.ds(0, 6 * COLS // X)], pass_send)
    drain(norm.at[0], norm_send)
    drain(adam_in.at[0], adam_send.at[0])
    drain(adam_in.at[pl.ds(0, 3)], adam_send.at[1])
    drain(adam_in.at[pl.ds(0, 3)], adam_send.at[2])
    drain(adam_in.at[pl.ds(0, 7)], adam_send.at[3])
    for k in range(2):
        around = lax.rem(g - 2 * core - k + X, X)
        for steps, blocks in ((0, 8), (1, 5), (2, 2), (3, 5)):

            @pl.when(around == steps)
            def _():
                drain(lroot.at[pl.ds(0, blocks * COLS // X)], root_send.at[k])

        around = lax.rem(2 * core + k - g + X, X)
        for which in range(2):

            @pl.when(lax.rem(around, 2) == 1)
            def _():
                drain(gleft.at[k], gram_send.at[which, k])

            @pl.when(around == 2)
            def _():
                drain(relay, gram_send.at[which, k])

    for which in range(2):
        drain(relay, relay_send.at[which])

    @pl.when(at_home)
    def _():
        drain(pieces.at[pl.ds(0, QUADS * X - 1)], out_send)

    @pl.when(jnp.logical_not(at_home))
    def _():
        drain(pieces, out_send)

    drain(returned, out_recv)

    def one_direction(b, carry):
        directions[b] = returned[slot_ref[b]]
        return carry

    lax.fori_loop(0, NBLK, one_direction, 0, unroll=8)


def hand_over(*refs):
    count = (len(refs) - 1) // 2
    sems = refs[-1]
    copies = [
        pltpu.make_async_copy(src, dst, sems.at[n])
        for n, (src, dst) in enumerate(zip(refs[:count], refs[count : 2 * count]))
    ]
    for copy in copies:
        copy.start()
    for copy in copies:
        copy.wait()


def run_exchange(grads, second_moment, slot_of, block_rows, block_cols, *matrices):
    half = jnp.bfloat16
    away = pl.BlockSpec(memory_space=pl.ANY)
    here = pl.BlockSpec(memory_space=pltpu.VMEM)
    numbers = pl.BlockSpec(memory_space=pltpu.SMEM)
    dma = pltpu.SemaphoreType.DMA
    operands = (slot_of, block_rows, block_cols, grads, second_moment, *matrices)
    results = pl.pallas_call(
        exchange,
        out_shape=(
            jax.ShapeDtypeStruct((NBLK, ROWS, COLS), half),
            jax.ShapeDtypeStruct((NBLK, ROWS, COLS), jnp.float32),
            jax.ShapeDtypeStruct((2, COLS, EDGE), jnp.float32),
            jax.ShapeDtypeStruct((2, COLS, EDGE), jnp.float32),
        ),
        in_specs=[numbers] * 3 + [away] * 6,
        out_specs=(here,) * 4,
        scratch_shapes=[
            pltpu.VMEM((QUADS * X, ROWS, COLS), half),
            pltpu.VMEM((NBLK + 1, ROWS, COLS), half),
            pltpu.VMEM((NBLK, ROWS, COLS), jnp.float32),
            pltpu.VMEM((8, 128), jnp.int32),
            pltpu.SMEM((8, 128), jnp.int32),
            pltpu.VMEM((NBLK, 128), jnp.int32),
            pltpu.VMEM((NBLK, 8, 128), jnp.float32),
            pltpu.VMEM((QUADS * X, ROWS, COLS), half),
            pltpu.VMEM((2, COLS, EDGE), half),
            pltpu.VMEM((2, COLS, EDGE), half),
            pltpu.VMEM((Z, Y, 2, ROWS, EDGE), half),
            pltpu.VMEM((EDGE, EDGE), half),
            pltpu.VMEM((EDGE, EDGE), half),
            pltpu.VMEM((Z, Y, 2, ROWS, HALF), half),
            pltpu.VMEM((EDGE, HALF), jnp.float32),
            pltpu.VMEM((QUADS * 2, ROWS, HALF), half),
            pltpu.VMEM((2, COLS, EDGE), half),
            pltpu.VMEM((2, COLS, EDGE), half),
            pltpu.VMEM((2, COLS, EDGE), jnp.float32),
            pltpu.VMEM((2, COLS, COLS), half),
            pltpu.VMEM((2, 2, COLS, COLS), half),
            pltpu.VMEM((14, 8, 128), jnp.float32),
            pltpu.VMEM((4, 8, 128), jnp.float32),
            pltpu.VMEM((2, 8, 128), jnp.float32),
            dma,
            dma((Y,)),
            dma,
            dma((Y,)),
            dma((2,)),
            dma,
            dma,
            dma,
            dma,
            dma((2, 2)),
            dma((2, 2)),
            dma((2,)),
            dma((2,)),
            dma((4,)),
            dma((4,)),
            dma,
            dma,
            dma,
            dma,
            dma((4,)),
            dma,
        ],
        compiler_params=pltpu.CompilerParams(
            collective_id=0, has_side_effects=True, vmem_limit_bytes=48 * 1024 * 1024
        ),
        cost_estimate=pl.CostEstimate(
            flops=8 * EDGE * EDGE * HALF, bytes_accessed=8 * EDGE * EDGE, transcendentals=0
        ),
    )(*[pltpu.with_memory_space_constraint(operand, pltpu.HBM) for operand in operands])
    return pl.pallas_call(
        hand_over,
        out_shape=[jax.ShapeDtypeStruct(result.shape, result.dtype) for result in results],
        in_specs=[here] * len(results),
        out_specs=[away] * len(results),
        scratch_shapes=[dma((len(results),))],
        compiler_params=pltpu.CompilerParams(vmem_limit_bytes=16 * 1024 * 1024),
    )(*results)


def solution(mesh):
    placed = (
        P(None, "fsdp", "group"),
        P(None, "fsdp", "group"),
        P(),
        P(),
        P(),
        P("fsdp", "group", None),
        P("fsdp", "group", None),
        P("fsdp", "group", None),
        P("fsdp", None, "group"),
    )
    return jax.shard_map(
        run_exchange,
        mesh=mesh,
        in_specs=placed,
        out_specs=(
            P(None, "fsdp", "group"),
            P(None, "fsdp", "group"),
            P("fsdp", "group", None),
            P("fsdp", "group", None),
        ),
        check_vma=False,
    )
```

```python
import jax
import jax.numpy as jnp
from jax import lax
from jax.experimental import pallas as pl
from jax.experimental.pallas import tpu as pltpu
from jax.sharding import PartitionSpec as P

MESH = pl.DeviceIdType.MESH
Z, Y, X = 8, 4, 4
QUADS = Z * Y
EDGE = 1024
NBLK = 56
HALF = EDGE // 2
ROWS, COLS = 16, 256
FAR_FIRST = (4, 3, 5, 2, 6, 1, 7, 0)


def drain(ref, sem):
    pltpu.make_async_copy(ref, ref, sem).wait()


def exchange(
    slot_ref,
    rows_ref,
    cols_ref,
    grads_ref,
    second_ref,
    lstat_ref,
    rstat_ref,
    lroot_ref,
    rroot_ref,
    directions,
    moments,
    new_left,
    new_right,
    returned,
    grads,
    second,
    table,
    table_smem,
    matches,
    adam_parts,
    pieces,
    gleft_in,
    gright_in,
    block,
    lroot,
    rroot,
    mixed,
    precond,
    direction,
    gleft,
    gright,
    gram_part,
    relay,
    cross,
    adam_in,
    adam_sum,
    norm,
    block_send,
    block_recv,
    swap_send,
    swap_recv,
    root_send,
    root_recv,
    row_recv,
    pass_send,
    pass_recv,
    gram_send,
    gram_recv,
    relay_send,
    relay_recv,
    adam_send,
    adam_recv,
    norm_send,
    norm_recv,
    out_send,
    out_recv,
    load_sem,
    table_sem,
):
    f = lax.axis_index("fsdp")
    g = lax.axis_index("group")
    core = lax.rem(f, 2)
    quad = lax.div(f, 2)
    y = lax.rem(quad, Y)
    z = lax.div(quad, Y)
    slot = quad * X + g
    other = f + 1 - 2 * core
    side = lax.div(g, 2)
    parity = lax.rem(g, 2)
    at_home = side == core

    def device(zz, yy, cc):
        return (zz * Y + yy) * 2 + cc

    def remote(src, dst, send, recv, ff, gg):
        pltpu.make_async_remote_copy(
            src_ref=src,
            dst_ref=dst,
            send_sem=send,
            recv_sem=recv,
            device_id=(ff, gg),
            device_id_type=MESH,
        ).start()

    def span(j):
        return pl.ds(pl.multiple_of(lax.rem(j, X) * COLS, COLS), COLS)

    def left_block(ref, j, k):
        return ref.at[span(j), span(k)]

    def send_root(k, ff, xx, lefts, rights):
        for d in lefts:
            src = lroot_ref.at[k, :, span(g + d)]
            remote(src, left_block(lroot, g, g + d), root_send.at[k], root_recv, ff, xx)
        for d in rights:
            src = rroot_ref.at[k, span(g + d), :]
            remote(src, left_block(rroot, g + d, g), root_send.at[k], root_recv, ff, xx)

    def send_roots():
        for k in range(2):
            home = 2 * core + k
            around = lax.rem(g - home + X, X)

            @pl.when(around == 0)
            def _():
                for src, dst in ((lroot_ref.at[k], lroot.at[span(g)]), (rroot_ref.at[k], rroot.at[:, span(g)])):
                    remote(src, dst, root_send.at[k], row_recv, other, g)
                    pltpu.make_async_copy(src, dst, row_recv).start()

            @pl.when(around == 1)
            def _():
                send_root(k, quad * 2, home, (0, 1, 2), (0, 1))

            @pl.when(around == 2)
            def _():
                send_root(k, quad * 2, home, (0,), ())
                send_root(k, quad * 2 + 1, home, (), (0,))

            @pl.when(around == 3)
            def _():
                send_root(k, quad * 2 + 1, home, (0, 3), (0, 3, 2))

    load_grads = pltpu.make_async_copy(grads_ref, grads.at[pl.ds(0, NBLK)], load_sem.at[0])
    load_second = pltpu.make_async_copy(second_ref, second, load_sem.at[1])
    load_left = pltpu.make_async_copy(lstat_ref, new_left, load_sem.at[2])
    load_right = pltpu.make_async_copy(rstat_ref, new_right, load_sem.at[3])
    load_grads.start()
    load_second.start()
    barrier = pltpu.get_barrier_semaphore()

    def greet(ff, gg):
        pl.semaphore_signal(barrier, inc=1, device_id=(ff, gg), device_id_type=MESH)

    for d in range(X):
        greet(other, lax.rem(g + d, X))
        if d:
            greet(f, lax.rem(g + d, X))

    @pl.loop(1, QUADS)
    def _(n):
        for d in range(X):
            greet(lax.rem(quad + n, QUADS) * 2 + core, lax.rem(g + d, X))

    lane = lax.broadcasted_iota(jnp.int32, (8, 128), 1)

    def valid(b):
        return (f * ROWS < rows_ref[b]) & (g * COLS < cols_ref[b])

    source = jnp.full((8, 128), NBLK, jnp.int32)
    for b in range(NBLK):
        match = lane == slot_ref[b]
        source = jnp.where(match, jnp.where(valid(b), b, NBLK), source)
        matches[pl.ds(b, 1)] = match[0:1].astype(jnp.int32)
    table[...] = source
    to_smem = pltpu.make_async_copy(table, table_smem, table_sem)
    to_smem.start()
    grads[NBLK] = jnp.zeros((ROWS, COLS), jnp.bfloat16)
    to_smem.wait()
    load_grads.wait()

    mine = block.at[z, y, core, :, pl.ds(pl.multiple_of(g * COLS, COLS), COLS)]

    @pl.loop(0, QUADS * X // 8)
    def _(n):
        for k in range(8):
            pieces[n * 8 + k] = grads[table_smem[0, n * 8 + k]]

    pl.semaphore_wait(barrier, QUADS * X + 3)
    send_roots()

    def send_blocks(step, carry):
        dy, dx = lax.div(step, X), lax.rem(step, X)
        yy, xx = lax.rem(y + dy, Y), lax.rem(g + dx, X)
        for dz in FAR_FIRST:
            zz = lax.rem(z + dz, Z)
            at = (zz * Y + yy) * X + xx
            src = pieces.at[at]
            if dz:
                remote(src, mine, block_send, block_recv.at[dy], device(zz, yy, core), xx)
            else:

                @pl.when(step == 0)
                def _():
                    pltpu.make_async_copy(src, mine, block_recv.at[0]).start()

                @pl.when(step != 0)
                def _():
                    remote(src, mine, block_send, block_recv.at[dy], device(zz, yy, core), xx)

        return carry

    lax.fori_loop(0, X * Y, send_blocks, 0)

    load_left.start()
    load_right.start()

    load_second.wait()

    def one_block(b, carry):
        grad = jnp.where(valid(b), grads[b].astype(jnp.float32), 0.0)
        moment = 0.95 * second[b] + 0.05 * grad * grad
        moments[b] = moment
        adam = grad / (jnp.sqrt(moment) + 1e-08)
        adam = adam * adam
        adam = adam[0:8] + adam[8:16]
        adam_parts[b] = adam[:, 0:128] + adam[:, 128:256]
        return carry

    lax.fori_loop(0, NBLK, one_block, 0, unroll=4)
    adam = jnp.sum(jnp.sum(adam_parts[...], axis=1), axis=1, keepdims=True)
    adam = jnp.where(matches[...] != 0, adam, 0.0)
    adam_sum[0] = jnp.broadcast_to(jnp.sum(adam, axis=0, keepdims=True), (8, 128))

    def adam_stage(stage, first, peers):
        for d, (ff, gg) in enumerate(peers):
            remote(adam_sum.at[stage], adam_in.at[first + d], adam_send.at[stage], adam_recv.at[stage], ff, gg)

    def adam_add(stage, first, count):
        drain(adam_in.at[pl.ds(first, count)], adam_recv.at[stage])
        total = adam_sum[stage]
        for d in range(count):
            total = total + adam_in[first + d]
        return total

    adam_stage(0, 0, [(other, g)])

    def pass_on(ref, j, k):
        here = left_block(ref, j, k)
        remote(here, here, pass_send, pass_recv, other, g)

    drain(lroot.at[pl.ds(0, 6 * COLS // X)], root_recv)

    @pl.when(core == 0)
    def _():
        for ref, j, k in ((lroot, 1, 1), (lroot, 1, 2), (lroot, 1, 3), (lroot, 2, 2), (rroot, 1, 1), (rroot, 2, 1)):
            pass_on(ref, g + j, g + k)

    @pl.when(core == 1)
    def _():
        for ref, j, k in ((lroot, 3, 3), (lroot, 3, 2), (rroot, 3, 3), (rroot, 2, 3), (rroot, 1, 3), (rroot, 2, 2)):
            pass_on(ref, g + j, g + k)

    adam_sum[1] = adam_add(0, 0, 1)
    adam_stage(1, 1, [(f, lax.rem(g + d, X)) for d in range(1, X)])

    drain(lroot.at[pl.ds(0, 2 * COLS)], row_recv)
    drain(lroot.at[pl.ds(0, 6 * COLS // X)], pass_recv)
    for j, k in ((1, 0), (2, 0), (3, 0), (2, 1), (2, 3), (1, 3)):
        rroot[span(g + k), span(g + j)] = rroot[span(g + j), span(g + k)].T
    for j, k in ((0, 1), (0, 2), (0, 3), (1, 2), (3, 2), (1, 3)):
        lroot[span(g + k), span(g + j)] = lroot[span(g + j), span(g + k)].T
    half = pl.ds(pl.multiple_of(core * HALF, HALF), HALF)

    def send_gram(which, m, src, dst):
        xx = 2 * core + m
        ff = quad * 2 + side
        around = lax.rem(xx - g + X, X)
        send = gram_send.at[which, m]

        @pl.when(around == 0)
        def _():
            pltpu.make_async_copy(src.at[m], dst.at[parity], gram_recv.at[which, parity]).start()

        @pl.when(lax.rem(around, 2) == 1)
        def _():
            remote(src.at[m], dst.at[parity], send, gram_recv.at[which, parity], ff, xx)

        @pl.when(around == 2)
        def _():
            for d, gg in ((0, lax.rem(g + 1, X)), (2, lax.rem(g + 3, X))):
                remote(src.at[m, :, span(g + d)], relay.at[which], send, relay_recv.at[which], ff, gg)

    def swap(d):
        ys = lax.rem(y + Y - d, Y)
        rows = block.at[:, ys, core]
        drain(rows, block_recv.at[d])
        remote(rows, rows, swap_send, swap_recv.at[d], other, g)

    def group(d):
        ys = lax.rem(y + Y - d, Y)
        drain(block.at[:, ys, 1 - core], swap_recv.at[d])
        for m in range(2):
            at = pl.multiple_of(core * HALF + m * COLS, COLS)
            value = lax.dot_general(
                block[:, ys, :, :, pl.ds(at, COLS)].reshape(COLS, COLS),
                block[:, ys].reshape(COLS, EDGE),
                (((0,), (0,)), ((), ())),
                preferred_element_type=jnp.float32,
            )
            if d:
                value = gram_part[m] + value
            if d < Y - 1:
                gram_part[m] = value
            else:
                gright[m] = value.astype(jnp.bfloat16)
                send_gram(1, m, gright, gright_in)
        value = jnp.dot(
            block[:, ys].reshape(COLS, EDGE), rroot[:, half], preferred_element_type=jnp.float32
        )
        mixed[:, ys] = value.astype(jnp.bfloat16).reshape(Z, 2, ROWS, HALF)

    swap(0)
    swap(1)
    group(0)
    swap(2)
    group(1)
    swap(3)
    group(2)
    group(3)

    adam_sum[2] = adam_add(1, 1, X - 1)
    adam_stage(2, 4, [(device(z, lax.rem(y + d, Y), core), g) for d in range(1, Y)])

    rows_valid, cols_valid = 0, 0
    for b in range(NBLK):
        rows_valid = jnp.where(slot_ref[b] == slot, rows_ref[b], rows_valid)
        cols_valid = jnp.where(slot_ref[b] == slot, cols_ref[b], cols_valid)
    cols_keep = (core * HALF + lax.broadcasted_iota(jnp.int32, (COLS, HALF), 1)) < cols_valid

    def one_part(m, total):
        at = pl.multiple_of(m * COLS, COLS)
        value = jnp.dot(lroot[pl.ds(at, COLS)], mixed[...].reshape(EDGE, HALF), preferred_element_type=jnp.float32)
        rows_keep = (at + lax.broadcasted_iota(jnp.int32, (COLS, HALF), 0)) < rows_valid
        value = jnp.where(rows_keep & cols_keep, value, 0.0)
        precond[pl.ds(at, COLS)] = value
        square = value * value
        return total + jnp.sum(square.reshape(COLS // 8, 8, HALF), axis=0)

    total = lax.fori_loop(0, 4, one_part, jnp.zeros((8, HALF), jnp.float32))
    norm[0] = jnp.broadcast_to(jnp.sum(total, keepdims=True), (8, 128))
    remote(norm.at[0], norm.at[1], norm_send, norm_recv, other, g)

    adam_sum[3] = adam_add(2, 4, Y - 1)
    adam_stage(3, 7, [(device(lax.rem(z + d, Z), y, core), g) for d in range(1, Z)])

    for m in range(2):
        gleft[m] = lax.dot_general(
            block[pl.ds(core * 4 + m * 2, 2)].reshape(COLS, EDGE),
            block[...].reshape(EDGE, EDGE),
            (((1,), (1,)), ((), ())),
            preferred_element_type=jnp.float32,
        ).astype(jnp.bfloat16)
        send_gram(0, m, gleft, gleft_in)

    adam = adam_add(3, 7, Z - 1)
    adam = jnp.sum(jnp.where(lane == slot, adam, 0.0)[0:1], keepdims=True)

    drain(norm.at[1], norm_recv)
    squares = (norm[0] + norm[1])[0:1, 0:1]
    factor = jnp.sqrt(adam) / (jnp.sqrt(squares) + 1e-06)

    @pl.loop(0, 4)
    def _(m):
        at = pl.multiple_of(m * COLS, COLS)
        value = (precond[pl.ds(at, COLS)] * factor).astype(jnp.bfloat16)
        direction[pl.ds(m * 16, 16)] = value.reshape(16, ROWS, HALF)

    def send_out(step, carry):
        dy, dc, e = lax.div(step, 4), lax.rem(lax.div(step, 2), 2), lax.rem(step, 2)
        yy, cc, xx = lax.rem(y + dy, Y), lax.rem(core + dc, 2), 2 * core + e
        for dz in FAR_FIRST:
            ff = device(lax.rem(z + dz, Z), yy, cc)
            src = direction.at[ff, :, pl.ds(pl.multiple_of(e * COLS, COLS), COLS)]
            dst = returned.at[slot]
            if dz:
                remote(src, dst, out_send, out_recv, ff, xx)
            else:
                local = (step < 2) & at_home & (parity == e)

                @pl.when(local)
                def _():
                    pltpu.make_async_copy(src, dst, out_recv).start()

                @pl.when(jnp.logical_not(local))
                def _():
                    remote(src, dst, out_send, out_recv, ff, xx)

        return carry

    lax.fori_loop(0, 16, send_out, 0)

    arounds = [lax.rem(g - 2 * core - k + X, X) for k in range(2)]
    for which, gram in ((1, gright_in), (0, gleft_in)):
        for k in range(2):
            for way in (1, 3):

                @pl.when(arounds[k] == way)
                def _():
                    drain(gram.at[k], gram_recv.at[which, k])
                    drain(relay.at[which], relay_recv.at[which])
                    gg = lax.rem(g + way, X)
                    here = gram.at[k, :, span(g + way)]
                    send = relay_send.at[which]
                    recv = gram_recv.at[which, k]
                    remote(here, cross.at[which, way // 2], send, recv, f, gg)
                    column = span(g + 3)
                    remote(relay.at[which], gram.at[k, :, column], send, recv, f, gg)

    def update(target, gram, k):
        @pl.loop(0, 8)
        def _(m):
            at = pl.ds(pl.multiple_of(m * 32, 32), 32)
            target[k, at] = 0.9 * target[k, at] + 0.1 * gram[k, at].astype(jnp.float32)

    parts = ((1, new_right, gright_in), (0, new_left, gleft_in))
    load_left.wait()
    load_right.wait()
    for last in (False, True):
        for which, target, gram in parts:
            for k in range(2):

                @pl.when((arounds[k] == 2) == last)
                def _():
                    if last:
                        drain(gram.at[k], gram_recv.at[which, k])
                        gram[k, :, span(g + 3)] = cross[which, 0].T
                        gram[k, :, span(g + 1)] = cross[which, 1].T
                    else:

                        @pl.when(arounds[k] == 0)
                        def _():
                            drain(gram.at[k], gram_recv.at[which, k])

                    update(target, gram, k)

    drain(pieces.at[pl.ds(0, QUADS * X - 1)], block_send)
    drain(pieces, swap_send)
    drain(lroot.at[pl.ds(0, 6 * COLS // X)], pass_send)
    drain(norm.at[0], norm_send)
    drain(adam_in.at[0], adam_send.at[0])
    drain(adam_in.at[pl.ds(0, 3)], adam_send.at[1])
    drain(adam_in.at[pl.ds(0, 3)], adam_send.at[2])
    drain(adam_in.at[pl.ds(0, 7)], adam_send.at[3])
    for k in range(2):
        around = lax.rem(g - 2 * core - k + X, X)
        for steps, blocks in ((0, 8), (1, 5), (2, 2), (3, 5)):

            @pl.when(around == steps)
            def _():
                drain(lroot.at[pl.ds(0, blocks * COLS // X)], root_send.at[k])

        around = lax.rem(2 * core + k - g + X, X)
        for which in range(2):

            @pl.when(lax.rem(around, 2) == 1)
            def _():
                drain(gleft.at[k], gram_send.at[which, k])

            @pl.when(around == 2)
            def _():
                drain(relay, gram_send.at[which, k])

    for which in range(2):
        drain(relay, relay_send.at[which])

    @pl.when(at_home)
    def _():
        drain(pieces.at[pl.ds(0, QUADS * X - 1)], out_send)

    @pl.when(jnp.logical_not(at_home))
    def _():
        drain(pieces, out_send)

    drain(returned, out_recv)

    def one_direction(b, carry):
        directions[b] = returned[slot_ref[b]]
        return carry

    lax.fori_loop(0, NBLK, one_direction, 0, unroll=8)


def hand_over(*refs):
    count = (len(refs) - 1) // 2
    sems = refs[-1]
    copies = [
        pltpu.make_async_copy(src, dst, sems.at[n])
        for n, (src, dst) in enumerate(zip(refs[:count], refs[count : 2 * count]))
    ]
    for copy in copies:
        copy.start()
    for copy in copies:
        copy.wait()


def run_exchange(grads, second_moment, slot_of, block_rows, block_cols, *matrices):
    half = jnp.bfloat16
    away = pl.BlockSpec(memory_space=pl.ANY)
    here = pl.BlockSpec(memory_space=pltpu.VMEM)
    numbers = pl.BlockSpec(memory_space=pltpu.SMEM)
    dma = pltpu.SemaphoreType.DMA
    operands = (slot_of, block_rows, block_cols, grads, second_moment, *matrices)
    results = pl.pallas_call(
        exchange,
        out_shape=(
            jax.ShapeDtypeStruct((NBLK, ROWS, COLS), half),
            jax.ShapeDtypeStruct((NBLK, ROWS, COLS), jnp.float32),
            jax.ShapeDtypeStruct((2, COLS, EDGE), jnp.float32),
            jax.ShapeDtypeStruct((2, COLS, EDGE), jnp.float32),
        ),
        in_specs=[numbers] * 3 + [away] * 6,
        out_specs=(here,) * 4,
        scratch_shapes=[
            pltpu.VMEM((QUADS * X, ROWS, COLS), half),
            pltpu.VMEM((NBLK + 1, ROWS, COLS), half),
            pltpu.VMEM((NBLK, ROWS, COLS), jnp.float32),
            pltpu.VMEM((8, 128), jnp.int32),
            pltpu.SMEM((8, 128), jnp.int32),
            pltpu.VMEM((NBLK, 128), jnp.int32),
            pltpu.VMEM((NBLK, 8, 128), jnp.float32),
            pltpu.VMEM((QUADS * X, ROWS, COLS), half),
            pltpu.VMEM((2, COLS, EDGE), half),
            pltpu.VMEM((2, COLS, EDGE), half),
            pltpu.VMEM((Z, Y, 2, ROWS, EDGE), half),
            pltpu.VMEM((EDGE, EDGE), half),
            pltpu.VMEM((EDGE, EDGE), half),
            pltpu.VMEM((Z, Y, 2, ROWS, HALF), half),
            pltpu.VMEM((EDGE, HALF), jnp.float32),
            pltpu.VMEM((QUADS * 2, ROWS, HALF), half),
            pltpu.VMEM((2, COLS, EDGE), half),
            pltpu.VMEM((2, COLS, EDGE), half),
            pltpu.VMEM((2, COLS, EDGE), jnp.float32),
            pltpu.VMEM((2, COLS, COLS), half),
            pltpu.VMEM((2, 2, COLS, COLS), half),
            pltpu.VMEM((14, 8, 128), jnp.float32),
            pltpu.VMEM((4, 8, 128), jnp.float32),
            pltpu.VMEM((2, 8, 128), jnp.float32),
            dma,
            dma((Y,)),
            dma,
            dma((Y,)),
            dma((2,)),
            dma,
            dma,
            dma,
            dma,
            dma((2, 2)),
            dma((2, 2)),
            dma((2,)),
            dma((2,)),
            dma((4,)),
            dma((4,)),
            dma,
            dma,
            dma,
            dma,
            dma((4,)),
            dma,
        ],
        compiler_params=pltpu.CompilerParams(
            collective_id=0, has_side_effects=True, vmem_limit_bytes=48 * 1024 * 1024
        ),
        cost_estimate=pl.CostEstimate(
            flops=8 * EDGE * EDGE * HALF, bytes_accessed=8 * EDGE * EDGE, transcendentals=0
        ),
    )(*[pltpu.with_memory_space_constraint(operand, pltpu.HBM) for operand in operands])
    return pl.pallas_call(
        hand_over,
        out_shape=[jax.ShapeDtypeStruct(result.shape, result.dtype) for result in results],
        in_specs=[here] * len(results),
        out_specs=[away] * len(results),
        scratch_shapes=[dma((len(results),))],
        compiler_params=pltpu.CompilerParams(vmem_limit_bytes=16 * 1024 * 1024),
    )(*results)


def solution(mesh):
    placed = (
        P(None, "fsdp", "group"),
        P(None, "fsdp", "group"),
        P(),
        P(),
        P(),
        P("fsdp", "group", None),
        P("fsdp", "group", None),
        P("fsdp", "group", None),
        P("fsdp", None, "group"),
    )
    return jax.shard_map(
        run_exchange,
        mesh=mesh,
        in_specs=placed,
        out_specs=(
            P(None, "fsdp", "group"),
            P(None, "fsdp", "group"),
            P("fsdp", "group", None),
            P("fsdp", "group", None),
        ),
        check_vma=False,
    )
```
